32 devices in a mesh: branch: 4 (over y, core), shard: 8 (over z, x).
Axes of the slice: x: 2, y: 2, z: 4, core: 2. Of those that a mesh axis runs over, the one named last changes fastest.
Arguments:
- tokens: bfloat16 [128, 4096], P(('branch', 'shard')), may hold values from -6 to 6
- routes: int32 [128, 2], P(('branch', 'shard')), may hold values from 0 to 3, all different within a row; in each aligned block of 4 rows (0 to 3, 4 to 7, ...) at most 3 rows name the same one
- mixing: float32 [128, 2], P(('branch', 'shard')), may hold values from 0.2 to 1
- gate_weight: bfloat16 [4, 4096, 14336], P('branch', 'shard'), may hold values from -0.09375 to 0.09375
- up_weight: bfloat16 [4, 4096, 14336], P('branch', 'shard'), may hold values from -0.09375 to 0.09375
- down_weight: bfloat16 [4, 14336, 4096], P('branch', 'shard'), may hold values from -0.046875 to 0.046875
- key_value: bfloat16 [4, 4096, 2048], P('branch', 'shard'), may hold values from -6 to 6
Outputs:
- mixed_out: bfloat16 [128, 4096], P(('branch', 'shard'))
- merged_kv: bfloat16 [4096, 2048], P('shard', 'branch')
The draws below stay inside these ranges and needn't reach their ends.
Inputs may be any that keep to these rules, and one draw needn't show every extreme that they name: `routes`: in each block of the 4 tokens of one device no expert is named by more than 3 pairs, and in some block one expert is named by exactly 3; a token's two experts differ.
All inputs are finite; a program needn't handle non-finite values.
Results may differ from the reference program's by a relative error of at most 0.018.
Values may be sent and summed in bfloat16 or wider, within the bound.
No kernel may reach another device: no remote copies, remote signals or barrier semaphores. Data moves between devices by JAX's collectives and lax.ppermute only.
A program may use at most 192 MiB of HBM per device.

```python
import math
import jax
import jax.numpy as jnp
import numpy as np
from jax import lax

D = 4096
FF = 14336
KVW = 2048
TOK_DEV = 4
EXPERTS = 4
CAP = 3
TOKENS = 128
N_BRANCH = 4
N_SHARD = 8


def block_levels(rng, dims, cuts, smallest, largest):
    level = 1.0
    for dim, parts in cuts:
        draws = jax.random.uniform(jax.random.fold_in(jax.random.fold_in(rng, 6), dim), (parts,), jnp.float32, smallest / len(cuts), largest / len(cuts))
        level = level * jnp.repeat(jnp.exp(draws), dims[dim] // parts).reshape((-1,) + (1,) * (len(dims) - 1 - dim))
    return level


def assign_block(key, own, number, rows, count, top, reach, slope):
    sequence = jax.random.permutation(key, count)
    packed, usual = load_shares(count, rows * top, reach, slope, True), load_shares(count, rows * top, reach, slope, False)
    places = jnp.arange(count)

    def named(tallies, turn):
        used = int((tallies > 0).sum())
        fixed = max(1, used // 4)
        shifted = fixed + (places - fixed + turn * (used - fixed)) % max(1, count - fixed)
        return jnp.zeros((count,), jnp.int32).at[sequence[jnp.where(places < fixed, places, shifted)]].set(jnp.asarray(tallies, jnp.int32))

    tallies = jnp.where(number % 4 == 0, named(packed, number // 4), named(usual, number - number // 4 - 1))
    mixed = jax.random.permutation(jax.random.fold_in(own, 3), count)
    donor, receiver = mixed[0:count // 2 * 2:2], mixed[1:count // 2 * 2:2]
    room = jnp.minimum(tallies[donor] - 1, reach - tallies[receiver]) // 2
    room = jnp.where((donor == sequence[0]) | (receiver == sequence[0]) | (tallies[receiver] == 0), 0, jnp.maximum(room, 0))
    shifted = jax.random.randint(jax.random.fold_in(own, 4), (count // 2,), 0, 1 << 20) % (room + 1)
    tallies = tallies.at[donor].add(-shifted).at[receiver].add(shifted)
    labels = jnp.searchsorted(jnp.cumsum(tallies), jnp.arange(rows * top), side="right").astype(jnp.int32)
    table = labels.reshape(top, rows).T
    table = table[jax.random.permutation(jax.random.fold_in(own, 1), rows)]
    turn = jax.random.randint(jax.random.fold_in(own, 2), (rows, 1), 0, top)
    return jnp.take_along_axis(table, (jnp.arange(top)[None, :] + turn) % top, axis=1)


def load_shares(count, total, most, slope, full):
    loads = [(1 << 20) // math.isqrt(rank ** slope) + 1 for rank in range(1, count + 1)]
    largest = most if full else min(most, max(-(-total // count), total * loads[0] // sum(loads)))
    least = 1 if total - largest >= count - 1 else 0
    counts, spare = [largest] + [least] * (count - 1), total - largest - least * (count - 1)
    while spare > 0:
        candidates = [i for i in range(1, count) if counts[i] < largest] or [i for i in range(1, count) if counts[i] < most]
        pool, budget = sum([loads[i] for i in candidates]), spare
        for i in candidates:
            extra = min(most - counts[i], max(1, budget * loads[i] // pool), spare)
            counts[i] = counts[i] + extra
            spare = spare - extra
    return np.array(counts)


def centred(key, extent, scale, reach, shards=(), kind=jnp.bfloat16):
    loudness = block_levels(key, extent, shards, -0.22, 0.18) if shards else 1.0
    array = jax.random.normal(key, extent, jnp.float32) * scale * loudness
    return jnp.minimum(jnp.maximum(array, -reach), reach).astype(kind)


def setup_inputs(seed: int = 0) -> dict:
    keys = jax.random.split(jax.random.key(seed), 8)
    tokens = centred(keys[0], (TOKENS, D), 1.0, 6.0, ((0, 32),))
    routes_keys = jax.random.split(jax.random.fold_in(keys[1], 1), TOKENS // TOK_DEV)
    routes_turns = jax.random.permutation(jax.random.fold_in(keys[1], 3), TOKENS // TOK_DEV)
    routes = jax.vmap(lambda own, number: assign_block(jax.random.fold_in(keys[1], 2), own, number, TOK_DEV, EXPERTS, 2, CAP, 2))(routes_keys, routes_turns).reshape((TOKENS, 2))
    mixing = jnp.clip(0.2 + 0.8 * jax.random.uniform(keys[2], (TOKENS, 2), jnp.float32) ** block_levels(keys[2], (TOKENS, 2), ((0, 32),), -0.2, 0.2), 0.2, 1.0)
    gate_weight = centred(keys[3], (EXPERTS, D, FF), D ** -0.5, 0.09375, ((0, 4), (1, 8)))
    up_weight = centred(keys[4], (EXPERTS, D, FF), D ** -0.5, 0.09375, ((0, 4), (1, 8)))
    down_weight = centred(keys[5], (EXPERTS, FF, D), FF ** -0.5, 0.046875, ((0, 4), (1, 8)))
    key_value = centred(keys[6], (EXPERTS, D, KVW), 1.0, 6.0, ((0, 4), (1, 8)))
    return dict(tokens=tokens, routes=routes, mixing=mixing, gate_weight=gate_weight, up_weight=up_weight, down_weight=down_weight, key_value=key_value)


def reference(tokens, routes, mixing, gate_weight, up_weight, down_weight, key_value):
    device_count = N_BRANCH * N_SHARD
    pair_count = TOK_DEV * 2
    pair_ids = routes.reshape(device_count, pair_count).astype(jnp.int32)
    experts_row = jnp.arange(EXPERTS, dtype=jnp.int32)
    onehot = (pair_ids[:, :, None] == experts_row[None, None, :]).astype(jnp.int32)
    earlier = jnp.cumsum(onehot, axis=1) - onehot
    slots = jnp.sum(earlier * onehot, axis=2).astype(jnp.int32)
    devices = jnp.broadcast_to(jnp.arange(device_count, dtype=jnp.int32)[:, None], (device_count, pair_count))
    pair_index = jnp.arange(device_count * pair_count, dtype=jnp.int32).reshape(device_count, pair_count)
    table = jnp.zeros((EXPERTS, device_count, CAP), jnp.int32).at[pair_ids, devices, slots].set(pair_index)
    pair_tokens = jnp.repeat(tokens, 2, axis=0)
    slice_width = FF // N_SHARD

    def one_expert(expert):
        rows = pair_tokens[table[expert].reshape(-1)]
        gate = jnp.dot(rows, gate_weight[expert], preferred_element_type=jnp.float32)
        upper = jnp.dot(rows, up_weight[expert], preferred_element_type=jnp.float32)
        hidden = (jax.nn.silu(gate) * upper).astype(jnp.bfloat16)
        hidden_parts = hidden.reshape(rows.shape[0], N_SHARD, slice_width)
        down_parts = down_weight[expert].reshape(N_SHARD, slice_width, D)

        def add_part(total, index):
            piece = jnp.dot(hidden_parts[:, index, :], down_parts[index], preferred_element_type=jnp.float32)
            rounded = lax.optimization_barrier(piece.astype(jnp.bfloat16))
            return total + rounded.astype(jnp.float32), None

        total, unused = lax.scan(add_part, jnp.zeros((rows.shape[0], D), jnp.float32), jnp.arange(N_SHARD, dtype=jnp.int32))
        return total.astype(jnp.bfloat16).reshape(device_count, CAP, D)

    expert_rows = lax.map(one_expert, experts_row)
    picked = expert_rows[pair_ids, devices, slots].reshape(TOKENS, 2, D)
    mixed_out = jnp.sum(mixing[:, :, None] * picked.astype(jnp.float32), axis=1).astype(jnp.bfloat16)
    merged_kv = (jnp.sum(key_value.astype(jnp.float32), axis=0) / EXPERTS).astype(jnp.bfloat16)
    return mixed_out, merged_kv
```

```python
import jax
import jax.numpy as jnp
from jax import lax
from jax.sharding import PartitionSpec as P


def route_cells(routes, experts, capacity):
    pairs = routes.shape[0] * 2
    pair_ids = routes.reshape(pairs)
    onehot = (pair_ids[:, None] == jnp.arange(experts, dtype=jnp.int32)[None, :]).astype(jnp.int32)
    earlier = jnp.cumsum(onehot, axis=0) - onehot
    slots = jnp.sum(earlier * onehot, axis=1)
    cells = jnp.arange(experts * capacity, dtype=jnp.int32)
    return (pair_ids[None, :] == (cells // capacity)[:, None]) & (
        slots[None, :] == (cells % capacity)[:, None]
    )


def local(tokens, routes, mixing, gate_weight, up_weight, down_weight, key_value):
    experts = lax.axis_size("branch")
    shards = lax.axis_size("shard")
    token_count, width = tokens.shape
    capacity = max(2, (2 * token_count + experts - 1) // experts + 1)
    depth = gate_weight.shape[1]
    slice_width = down_weight.shape[1]
    placing = route_cells(routes, experts, capacity)
    pair_tokens = jnp.repeat(tokens, 2, axis=0)
    outgoing = jnp.dot(
        placing.astype(jnp.bfloat16), pair_tokens, preferred_element_type=jnp.float32
    ).astype(jnp.bfloat16)
    outgoing = outgoing.reshape(experts, capacity, shards, depth).transpose(0, 2, 1, 3)
    outgoing = outgoing.reshape(experts * shards, capacity, depth)
    pair_weights = placing.astype(jnp.float32).T * mixing.reshape(token_count * 2)[:, None]
    combine = jnp.sum(pair_weights.reshape(token_count, 2, experts * capacity), axis=1)

    arrived = lax.all_to_all(
        outgoing, ("branch", "shard"), split_axis=0, concat_axis=0, tiled=True
    )
    rows = arrived.reshape(-1, depth)
    count = rows.shape[0]
    gate = jnp.dot(rows, gate_weight[0], preferred_element_type=jnp.float32).astype(jnp.bfloat16)
    upper = jnp.dot(rows, up_weight[0], preferred_element_type=jnp.float32).astype(jnp.bfloat16)
    both = jnp.concatenate([gate, upper], axis=0)
    own = lax.psum_scatter(both, "shard", scatter_dimension=1, tiled=True).astype(jnp.float32)
    hidden = (jax.nn.silu(own[:count]) * own[count:]).astype(jnp.bfloat16)
    partial = jnp.dot(hidden, down_weight[0], preferred_element_type=jnp.float32)
    partial = partial.astype(jnp.bfloat16).reshape(experts, shards, capacity, width)
    partial = partial.transpose(1, 0, 2, 3).reshape(shards * experts * capacity, width)
    summed = lax.psum_scatter(partial, "shard", scatter_dimension=0, tiled=True)
    back = lax.all_to_all(
        summed.reshape(experts, capacity, width), "branch", split_axis=0, concat_axis=0, tiled=True
    )
    expert_flat = back.reshape(experts * capacity, width).astype(jnp.float32)
    mixed_out = jnp.dot(
        combine, expert_flat, precision=lax.Precision.HIGHEST, preferred_element_type=jnp.float32
    ).astype(jnp.bfloat16)

    merged = lax.psum_scatter(key_value[0], "branch", scatter_dimension=1, tiled=True)
    merged_kv = (merged.astype(jnp.float32) / experts).astype(jnp.bfloat16)
    return mixed_out, merged_kv


def solution(mesh):
    return jax.shard_map(
        local,
        mesh=mesh,
        in_specs=(
            P(("branch", "shard"), None),
            P(("branch", "shard"), None),
            P(("branch", "shard"), None),
            P("branch", "shard", None),
            P("branch", "shard", None),
            P("branch", "shard", None),
            P("branch", "shard", None),
        ),
        out_specs=(P(("branch", "shard"), None), P("shard", "branch")),
        check_vma=False,
    )
```

```python
import functools

import jax
import jax.numpy as jnp
from jax import lax
from jax.sharding import PartitionSpec as P

F32 = jnp.float32
BF16 = jnp.bfloat16


def ring_order(devices):
    places = [getattr(d, "coords", None) for d in devices]
    count = len(places)
    if any(p is None for p in places):
        return list(range(count))
    at = {(p[2], p[0]): i for i, p in enumerate(places)}
    zs, xs = sorted({k[0] for k in at}), sorted({k[1] for k in at})
    if len(at) != count or len(zs) * len(xs) != count or len(xs) < 2 or len(zs) % 2:
        return list(range(count))
    order = [at[(z, xs[0])] for z in zs]
    for i, z in enumerate(reversed(zs)):
        line = xs[1:] if i % 2 == 0 else list(reversed(xs[1:]))
        order += [at[(z, x)] for x in line]
    return order


def core_count(devices):
    places = [getattr(d, "coords", None) for d in devices]
    if any(p is None for p in places):
        return 1
    same = [tuple(p) == tuple(places[0]) for p in places]
    cores = sum(same)
    return cores if all(same[:cores]) and len(places) % cores == 0 else 1


def pick(x, index, axis):
    return lax.dynamic_index_in_dim(x, index, axis, keepdims=False)


def direct_sum(x, axis_name, me, count, target):
    total = pick(x, me, 0).astype(F32)
    for k in range(1, count):
        sent = pick(x, lax.rem(me + k, count), 0).astype(BF16)
        total = total + lax.ppermute(sent, axis_name, target(k)).astype(F32)
    return total


def branch_sum(x, cores):
    size = lax.axis_size("branch")
    chips = size // cores
    b = lax.axis_index("branch")
    core, chip = lax.rem(b, cores), lax.div(b, cores)
    x = jnp.swapaxes(x.reshape((chips, cores) + x.shape[1:]), 0, 1)
    x = direct_sum(
        x, "branch", core, cores,
        lambda k: [(i, i // cores * cores + (i + k) % cores) for i in range(size)],
    )
    return direct_sum(
        x, "branch", chip, chips,
        lambda k: [(i, (i + k * cores) % size) for i in range(size)],
    )


def cell_table(routes, mixing, experts, capacity):
    pairs = routes.shape[0] * 2
    ids = routes.reshape(pairs)
    order = jnp.arange(pairs, dtype=jnp.int32)
    same = (ids[:, None] == ids[None, :]) & (order[None, :] < order[:, None])
    slots = jnp.sum(same.astype(jnp.int32), axis=1)
    cells = jnp.arange(experts * capacity, dtype=jnp.int32)
    placing = cells[:, None] == (ids * capacity + slots)[None, :]
    number = jnp.sum(jnp.where(placing, order[None, :] // 2 + 1, 0), axis=1)
    weight = jnp.sum(jnp.where(placing, mixing.reshape(pairs)[None, :], 0.0), axis=1)
    return placing, number, weight


def local(order, cores, tokens, routes, mixing, gate_weight, up_weight, down_weight, key_value):
    experts = lax.axis_size("branch")
    shards = lax.axis_size("shard")
    token_count, width = tokens.shape
    capacity = max(2, (2 * token_count + experts - 1) // experts + 1)
    depth = gate_weight.shape[1]
    slice_width = down_weight.shape[1]
    count = experts * shards * capacity

    kv = key_value[0].reshape(key_value.shape[1], experts, -1).swapaxes(0, 1)
    merged_kv = (branch_sum(kv, cores) / experts).astype(BF16)

    placing, number, weight = cell_table(routes, mixing, experts, capacity)
    cells = jnp.dot(
        placing.astype(BF16), jnp.repeat(tokens, 2, axis=0), preferred_element_type=F32
    ).astype(BF16)
    high = weight.astype(BF16)
    low = (weight - high.astype(F32)).astype(BF16)
    extra = jnp.stack([number.astype(BF16), high, low], axis=1)
    extra = jnp.pad(extra, ((0, 0), (0, 125)))
    cells = jnp.concatenate([cells, extra], axis=1).reshape(experts, capacity, -1)
    cells = lax.all_to_all(cells, "branch", split_axis=0, concat_axis=0, tiled=True)
    cells = cells.reshape(experts * capacity, -1)
    body = cells[:, :width].reshape(experts * capacity, shards, depth).swapaxes(0, 1)
    tail = jnp.broadcast_to(cells[None, :, width:], (shards, experts * capacity, 128))
    cells = jnp.concatenate([body, tail], axis=2)
    cells = lax.all_to_all(cells, "shard", split_axis=0, concat_axis=0, tiled=True)
    cells = cells.reshape(count, depth + 128)
    rows = cells[:, :depth]
    number = cells[:, depth].astype(jnp.int32)
    weight = (cells[:, depth + 1].astype(F32) + cells[:, depth + 2].astype(F32))[:, None]

    gate = jnp.dot(rows, gate_weight[0], preferred_element_type=F32)
    upper = jnp.dot(rows, up_weight[0], preferred_element_type=F32)

    place = [0] * shards
    for i, s in enumerate(order):
        place[s] = i
    here = jnp.asarray(place, jnp.int32)[lax.axis_index("shard")]
    owner = jnp.asarray(order, jnp.int32)
    forth = [(order[i], order[(i + 1) % shards]) for i in range(shards)]
    back = [(b, a) for a, b in forth]

    def piece(x, step):
        who = owner[lax.rem(here + step + 2 * shards, shards)]
        return lax.dynamic_slice_in_dim(x, who * slice_width, slice_width, 1)

    gate_sum, up_sum = piece(gate, -1), piece(upper, 1)
    for t in range(1, shards):
        gate_in = lax.ppermute(gate_sum.astype(BF16), "shard", forth)
        up_in = lax.ppermute(up_sum.astype(BF16), "shard", back)
        gate_sum = gate_in.astype(F32) + piece(gate, -1 - t)
        up_sum = up_in.astype(F32) + piece(upper, 1 + t)

    hidden = (jax.nn.silu(gate_sum) * up_sum * weight).astype(BF16)
    cell = jnp.arange(count, dtype=jnp.int32)
    source = cell // capacity
    source = lax.rem(source, experts) * shards + source // experts
    target = jnp.where(number > 0, source * token_count + number - 1, -1)
    spread = target[:, None] == jnp.arange(experts * shards * token_count, dtype=jnp.int32)[None, :]
    hidden = lax.dot_general(
        spread.astype(BF16), hidden, (((0,), (0,)), ((), ())), preferred_element_type=F32
    ).astype(BF16)
    partial = jnp.dot(hidden, down_weight[0], preferred_element_type=F32)
    partial = branch_sum(partial.reshape(experts, shards * token_count, width), cores)
    partial = partial.astype(BF16).reshape(shards, token_count, width)
    partial = lax.all_to_all(partial, "shard", split_axis=0, concat_axis=0, tiled=True)
    mixed_out = jnp.sum(partial.astype(F32), axis=0).astype(BF16)
    return mixed_out, merged_kv


def solution(mesh):
    grid = mesh.devices
    order = ring_order(list(grid[0, :]))
    cores = core_count(list(grid[:, 0]))
    return jax.shard_map(
        functools.partial(local, order, cores),
        mesh=mesh,
        in_specs=(
            P(("branch", "shard"), None),
            P(("branch", "shard"), None),
            P(("branch", "shard"), None),
            P("branch", "shard", None),
            P("branch", "shard", None),
            P("branch", "shard", None),
            P("branch", "shard", None),
        ),
        out_specs=(P(("branch", "shard"), None), P("shard", "branch")),
        check_vma=False,
    )
```

```python
import functools

import jax
import jax.numpy as jnp
import numpy as np
from jax import lax
from jax.experimental import pallas as pl
from jax.experimental.pallas import tpu as pltpu
from jax.sharding import PartitionSpec as P

F32 = jnp.float32
BF16 = jnp.bfloat16
LANES = 128
VMEM_LIMIT = 40 * 1024 * 1024


def ring_order(devices):
    places = [getattr(d, "coords", None) for d in devices]
    count = len(places)
    if any(p is None for p in places):
        return list(range(count))
    at = {(p[2], p[0]): i for i, p in enumerate(places)}
    zs, xs = sorted({k[0] for k in at}), sorted({k[1] for k in at})
    if len(at) != count or len(zs) * len(xs) != count or len(xs) < 2 or len(zs) % 2:
        return list(range(count))
    order = [at[(z, xs[0])] for z in zs]
    for i, z in enumerate(reversed(zs)):
        line = xs[1:] if i % 2 == 0 else list(reversed(xs[1:]))
        order += [at[(z, x)] for x in line]
    return order


def core_count(devices):
    places = [getattr(d, "coords", None) for d in devices]
    if any(p is None for p in places):
        return 1
    same = [tuple(p) == tuple(places[0]) for p in places]
    cores = sum(same)
    return cores if all(same[:cores]) and len(places) % cores == 0 else 1


def turned(index, step, count):
    return lax.rem(index + step, jnp.int32(count))


def place_rows(tokens, routes, mixing, experts, capacity, shards):
    token_count, width = tokens.shape
    depth = width // shards
    padded = -(-capacity // 8) * 8

    def kernel(tokens_ref, routes_ref, mixing_ref, out_ref):
        ids = [routes_ref[p % 2, p // 2] for p in range(2 * token_count)]
        slots = []
        for p in range(2 * token_count):
            slot = jnp.int32(0)
            for q in range(p):
                slot = slot + jnp.where(ids[q] == ids[p], 1, 0)
            slots.append(slot)
        row = lax.broadcasted_iota(jnp.int32, (padded, LANES), 0)
        lane = lax.broadcasted_iota(jnp.int32, (padded, LANES), 1)
        values = tokens_ref[...].astype(F32)
        tails = []
        for p in range(2 * token_count):
            weight = jnp.full((padded, LANES), mixing_ref[p % 2, p // 2], F32)
            high = weight.astype(BF16).astype(F32)
            number = jnp.full((padded, LANES), float(p // 2 + 1), F32)
            tail = jnp.where(lane == 1, high, jnp.where(lane == 2, weight - high, 0.0))
            tails.append(jnp.where(lane == 0, number, tail))
        for e in range(experts):
            tail = jnp.zeros((padded, LANES), F32)
            body = jnp.zeros((padded, width), F32)
            for p in range(2 * token_count):
                slot = jnp.where(ids[p] == e, slots[p], -1)
                tail = jnp.where(row == slot, tails[p], tail)
                here = lax.broadcasted_iota(jnp.int32, (padded, width), 0) == slot
                t = p // 2
                body = jnp.where(here, jnp.broadcast_to(values[t : t + 1], (padded, width)), body)
            body, tail = body.astype(BF16)[:capacity], tail.astype(BF16)[:capacity]
            for s in range(shards):
                at = s * (depth + LANES)
                out_ref[e, :, at : at + depth] = body[:, s * depth : (s + 1) * depth]
                out_ref[e, :, at + depth : at + depth + LANES] = tail

    return pl.pallas_call(
        kernel,
        out_shape=jax.ShapeDtypeStruct((experts, capacity, shards * (depth + LANES)), BF16),
        in_specs=[
            pl.BlockSpec(memory_space=pltpu.VMEM),
            pl.BlockSpec(memory_space=pltpu.SMEM),
            pl.BlockSpec(memory_space=pltpu.SMEM),
        ],
        out_specs=pl.BlockSpec(memory_space=pltpu.VMEM),
        name="place_rows",
    )(tokens, routes.T, mixing.T)


def column_pieces(where, table, rows, gate_weight, up_weight, pieces, first, cuts, kind):
    count, depth = rows.shape
    shards = len(table) and int(np.sqrt(len(table) // 2))
    width = gate_weight.shape[2] // shards
    block = width // cuts
    chunk = block if block <= 256 else next(c for c in (256, 128) if block % c == 0)

    def kernel(where_ref, table_ref, rows_ref, gate_ref, up_ref, gate_out, up_out):
        held = rows_ref[...]
        for at in range(0, block, chunk):
            for ref, out in ((gate_ref, gate_out), (up_ref, up_out)):
                value = jnp.dot(held, ref[0, :, at : at + chunk], preferred_element_type=F32)
                out[0, :, at : at + chunk] = value.astype(kind)

    def weight_map(side):
        def index(i, j, where_ref, table_ref):
            return 0, 0, table_ref[(where_ref[1] * 2 + side) * shards + first + i] * cuts + j

        return index

    out = jax.ShapeDtypeStruct((pieces, count, width), kind)
    return pl.pallas_call(
        kernel,
        out_shape=(out, out),
        grid_spec=pltpu.PrefetchScalarGridSpec(
            num_scalar_prefetch=2,
            grid=(pieces, cuts),
            in_specs=[
                pl.BlockSpec((count, depth), lambda i, j, *_: (0, 0)),
                pl.BlockSpec((1, depth, block), weight_map(0)),
                pl.BlockSpec((1, depth, block), weight_map(1)),
            ],
            out_specs=[pl.BlockSpec((1, count, block), lambda i, j, *_: (i, 0, j))] * 2,
        ),
        compiler_params=pltpu.CompilerParams(vmem_limit_bytes=VMEM_LIMIT),
        cost_estimate=pl.CostEstimate(
            flops=4 * pieces * count * depth * width,
            bytes_accessed=4 * pieces * depth * width,
            transcendentals=0,
        ),
        name="column_pieces",
    )(where, jnp.asarray(table, jnp.int32), rows, gate_weight, up_weight)


def plain_pieces(here, table, rows, gate_weight, up_weight, shards):
    width = gate_weight.shape[2] // shards
    both = []
    for side, weight in enumerate((gate_weight, up_weight)):
        value = jnp.dot(rows, weight[0], preferred_element_type=F32)
        at = jnp.asarray(table, jnp.int32).reshape(shards, 2, shards)[here, side] * width
        both.append([lax.dynamic_slice_in_dim(value, at[t], width, 1) for t in range(shards)])
    return both


def turn_columns(where, x, cores, chips):
    rows, total = x.shape[1:]
    block = total // (cores * chips)

    def index(i, where_ref):
        b = where_ref[0]
        chip = turned(lax.div(b, jnp.int32(cores)), lax.rem(i, jnp.int32(chips)), chips)
        core = turned(lax.rem(b, jnp.int32(cores)), lax.div(i, jnp.int32(chips)), cores)
        return 0, 0, chip * cores + core

    def kernel(where_ref, in_ref, out_ref):
        out_ref[...] = in_ref[...]

    return pl.pallas_call(
        kernel,
        out_shape=jax.ShapeDtypeStruct((cores * chips, rows, block), x.dtype),
        grid_spec=pltpu.PrefetchScalarGridSpec(
            num_scalar_prefetch=1,
            grid=(cores * chips,),
            in_specs=[pl.BlockSpec((1, rows, block), index)],
            out_specs=pl.BlockSpec((1, rows, block), lambda i, *_: (i, 0, 0)),
        ),
        cost_estimate=pl.CostEstimate(flops=0, bytes_accessed=4 * rows * total, transcendentals=0),
        name="turn_columns",
    )(where, x)


def expert_outputs(where, gate_in, up_in, gate_own, up_own, tails, down_weight, sizes):
    experts, shards, cores, token_count, capacity = sizes
    chips = experts // cores
    count, slice_width = gate_in.shape
    width = down_weight.shape[2]
    total = experts * shards * token_count
    kept = total // cores
    block = 512 if width % 512 == 0 else width
    cell = np.arange(count)
    origin = np.zeros((count, LANES), np.float32)
    branch = cell % (experts * capacity) // capacity
    origin[:, 0] = branch // cores
    origin[:, 1] = branch % cores
    origin[:, 2] = cell // (experts * capacity) * token_count
    chunk = next(c for c in (256, 128, slice_width) if slice_width % c == 0)

    def kernel(where_ref, gate_ref, up_ref, gate_own_ref, up_own_ref, tail_ref, origin_ref, down_ref, *rest):
        hidden_ref = rest[-1]

        @pl.when(pl.program_id(0) == 0)
        def _():
            b = where_ref[0]
            tail = tail_ref[...].astype(F32)
            place = origin_ref[...]
            number, weight = tail[:, 0:1], tail[:, 1:2] + tail[:, 2:3]
            chip = place[:, 0:1] - lax.div(b, jnp.int32(cores)).astype(F32)
            core = place[:, 1:2] - lax.rem(b, jnp.int32(cores)).astype(F32)
            chip = jnp.where(chip < 0, chip + chips, chip)
            core = jnp.where(core < 0, core + cores, core)
            target = (core * chips + chip) * (shards * token_count) + place[:, 2:3] + number - 1.0
            target = jnp.where(number > 0, target, -1.0).astype(jnp.int32)
            spread = target == lax.broadcasted_iota(jnp.int32, (count, total), 1)
            spread = spread.astype(F32).astype(BF16)
            for at in range(0, slice_width, chunk):
                cut = slice(at, at + chunk)
                gate = gate_ref[:, cut].astype(F32) + gate_own_ref[:, cut]
                upper = up_ref[:, cut].astype(F32) + up_own_ref[:, cut]
                hidden = (gate / (1.0 + jnp.exp(-gate)) * upper * weight).astype(BF16)
                hidden_ref[:, cut] = lax.dot_general(
                    spread, hidden, (((0,), (0,)), ((), ())), preferred_element_type=F32
                ).astype(BF16)

        value = jnp.dot(hidden_ref[...], down_ref[0], preferred_element_type=F32)
        rest[0][...] = value[:kept]
        if cores > 1:
            rest[1][...] = value[kept:].astype(BF16)

    whole = pl.BlockSpec((count, slice_width), lambda j, *_: (0, 0))
    lanes = pl.BlockSpec((count, LANES), lambda j, *_: (0, 0))
    shapes = [jax.ShapeDtypeStruct((kept, width), F32)]
    specs = [pl.BlockSpec((kept, block), lambda j, *_: (0, j))]
    if cores > 1:
        shapes.append(jax.ShapeDtypeStruct((total - kept, width), BF16))
        specs.append(pl.BlockSpec((total - kept, block), lambda j, *_: (0, j)))
    return pl.pallas_call(
        kernel,
        out_shape=shapes,
        grid_spec=pltpu.PrefetchScalarGridSpec(
            num_scalar_prefetch=1,
            grid=(width // block,),
            in_specs=[
                whole, whole, whole, whole, lanes, lanes,
                pl.BlockSpec((1, slice_width, block), lambda j, *_: (0, 0, j)),
            ],
            out_specs=specs,
            scratch_shapes=[pltpu.VMEM((total, slice_width), BF16)],
        ),
        compiler_params=pltpu.CompilerParams(vmem_limit_bytes=VMEM_LIMIT),
        cost_estimate=pl.CostEstimate(
            flops=2 * total * slice_width * width,
            bytes_accessed=2 * slice_width * width,
            transcendentals=count * slice_width,
        ),
        name="expert_outputs",
    )(where, gate_in, up_in, gate_own, up_own, tails, jnp.asarray(origin), down_weight)


def core_target(size, cores, k):
    return [(i, i // cores * cores + (i + k) % cores) for i in range(size)]


def chip_target(size, cores, k):
    return [(i, (i + k * cores) % size) for i in range(size)]


def local(order, cores, tokens, routes, mixing, gate_weight, up_weight, down_weight, key_value):
    experts = lax.axis_size("branch")
    shards = lax.axis_size("shard")
    chips = experts // cores
    token_count, width = tokens.shape
    capacity = max(2, (2 * token_count + experts - 1) // experts + 1)
    depth = gate_weight.shape[1]
    slice_width = down_weight.shape[1]
    count = experts * shards * capacity
    where = jnp.stack([lax.axis_index("branch"), lax.axis_index("shard")]).astype(jnp.int32)

    place = np.argsort(np.asarray(order))
    table = np.zeros((shards, 2, shards), np.int32)
    for s in range(shards):
        for t in range(shards):
            table[s, 0, t] = order[(place[s] - 1 - t) % shards]
            table[s, 1, t] = order[(place[s] + 1 + t) % shards]
    table = table.reshape(-1)
    forth = [(order[i], order[(i + 1) % shards]) for i in range(shards)]
    back = [(b, a) for a, b in forth]

    cells = place_rows(tokens, routes, mixing, experts, capacity, shards)
    cells = lax.all_to_all(cells, "branch", split_axis=0, concat_axis=0, tiled=True)
    cells = cells.reshape(experts * capacity, shards, depth + LANES).swapaxes(0, 1)
    cells = lax.all_to_all(cells, "shard", split_axis=0, concat_axis=0, tiled=True)
    cells = cells.reshape(count, depth + LANES)
    rows, tails = cells[:, :depth], cells[:, depth:]

    kv = turn_columns(where, key_value, cores, chips)
    kv_rows, kv_block = kv.shape[1:]
    kv = kv.reshape(cores, chips, kv_rows, kv_block)

    if slice_width % LANES == 0:
        cuts = 2 if slice_width % (2 * LANES) == 0 else 1
        one = column_pieces(where, table, rows, gate_weight, up_weight, 1, 0, cuts, BF16)
        gate_sum, up_sum = one[0][0], one[1][0]
        gates, ups = column_pieces(
            where, table, rows, gate_weight, up_weight, shards - 1, 1, 1, F32
        )
    else:
        gates, ups = plain_pieces(where[1], table, rows, gate_weight, up_weight, shards)
        gate_sum, up_sum = gates.pop(0).astype(BF16), ups.pop(0).astype(BF16)

    kv_core = [
        lax.ppermute(kv[k], "branch", core_target(experts, cores, k)) for k in range(1, cores)
    ]
    kv_sum = None
    for t in range(1, shards):
        gate_in = lax.ppermute(gate_sum, "shard", forth)
        up_in = lax.ppermute(up_sum, "shard", back)
        if t == min(2, shards - 1):
            gate_in, kv_core = lax.optimization_barrier((gate_in, kv_core))
            kv_sum = kv[0].astype(F32) + sum(x.astype(F32) for x in kv_core)
            kv_chip = [
                lax.ppermute(kv_sum[k].astype(BF16), "branch", chip_target(experts, cores, k))
                for k in range(1, chips)
            ]
        if t == min(5, shards - 1):
            gate_in, kv_chip = lax.optimization_barrier((gate_in, kv_chip))
            kv_sum = kv_sum[0] + sum(x.astype(F32) for x in kv_chip)
            merged_kv = (kv_sum / experts).astype(BF16)
        if t < shards - 1:
            gate_sum = (gate_in.astype(F32) + gates[t - 1]).astype(BF16)
            up_sum = (up_in.astype(F32) + ups[t - 1]).astype(BF16)

    sizes = (experts, shards, cores, token_count, capacity)
    outputs = expert_outputs(
        where, gate_in, up_in, gates[shards - 2], ups[shards - 2], tails, down_weight, sizes
    )
    total = outputs[0].reshape(chips, shards * token_count, width)
    for k in range(1, cores):
        sent = outputs[1].reshape(cores - 1, chips, shards * token_count, width)[k - 1]
        total = total + lax.ppermute(sent, "branch", core_target(experts, cores, k)).astype(F32)
    mixed = total[0]
    for k in range(1, chips):
        sent = total[k].astype(BF16)
        mixed = mixed + lax.ppermute(sent, "branch", chip_target(experts, cores, k)).astype(F32)
    mixed = mixed.astype(BF16).reshape(shards, token_count, width)
    mixed = lax.all_to_all(mixed, "shard", split_axis=0, concat_axis=0, tiled=True)
    mixed_out = jnp.sum(mixed.astype(F32), axis=0).astype(BF16)
    return mixed_out, merged_kv


def solution(mesh):
    grid = mesh.devices
    order = ring_order(list(grid[0, :]))
    cores = core_count(list(grid[:, 0]))
    return jax.shard_map(
        functools.partial(local, order, cores),
        mesh=mesh,
        in_specs=(
            P(("branch", "shard"), None),
            P(("branch", "shard"), None),
            P(("branch", "shard"), None),
            P("branch", "shard", None),
            P("branch", "shard", None),
            P("branch", "shard", None),
            P("branch", "shard", None),
        ),
        out_specs=(P(("branch", "shard"), None), P("shard", "branch")),
        check_vma=False,
    )
```

```python
import functools

import jax
import jax.numpy as jnp
import numpy as np
from jax import lax
from jax.experimental import pallas as pl
from jax.experimental.pallas import tpu as pltpu
from jax.sharding import PartitionSpec as P

F32 = jnp.float32
BF16 = jnp.bfloat16
LANES = 128
VMEM_LIMIT = 40 * 1024 * 1024


def ring_order(devices):
    places = [getattr(d, "coords", None) for d in devices]
    count = len(places)
    if any(p is None for p in places):
        return list(range(count))
    at = {(p[2], p[0]): i for i, p in enumerate(places)}
    zs, xs = sorted({k[0] for k in at}), sorted({k[1] for k in at})
    if len(at) != count or len(zs) * len(xs) != count or len(xs) < 2 or len(zs) % 2:
        return list(range(count))
    order = [at[(z, xs[0])] for z in zs]
    for i, z in enumerate(reversed(zs)):
        line = xs[1:] if i % 2 == 0 else list(reversed(xs[1:]))
        order += [at[(z, x)] for x in line]
    return order


def core_count(devices):
    places = [getattr(d, "coords", None) for d in devices]
    if any(p is None for p in places):
        return 1
    same = [tuple(p) == tuple(places[0]) for p in places]
    cores = sum(same)
    return cores if all(same[:cores]) and len(places) % cores == 0 else 1


def turned(index, step, count):
    return lax.rem(index + step, jnp.int32(count))


def place_rows(where, tokens, routes, mixing, experts, cores, capacity, shards):
    token_count, width = tokens.shape
    depth = width // shards
    chips = experts // cores
    padded = -(-capacity // 8) * 8

    def kernel(where_ref, tokens_ref, routes_ref, mixing_ref, *outs):
        b, s = where_ref[0], where_ref[1]
        chip, core = lax.div(b, jnp.int32(cores)), lax.rem(b, jnp.int32(cores))
        ids = [routes_ref[p % 2, p // 2] for p in range(2 * token_count)]
        slots = []
        for p in range(2 * token_count):
            slot = jnp.int32(0)
            for q in range(p):
                slot = slot + jnp.where(ids[q] == ids[p], 1, 0)
            slots.append(slot)
        row = lax.broadcasted_iota(jnp.int32, (padded, LANES), 0)
        lane = lax.broadcasted_iota(jnp.int32, (padded, LANES), 1)
        wide_row = lax.broadcasted_iota(jnp.int32, (padded, depth), 0)
        tails = []
        for p in range(2 * token_count):
            weight = jnp.full((padded, LANES), mixing_ref[p % 2, p // 2], F32)
            high = weight.astype(BF16).astype(F32)
            number = jnp.full((padded, LANES), float(p // 2 + 1), F32)
            tail = jnp.where(lane == 1, high, jnp.where(lane == 2, weight - high, 0.0))
            tails.append(jnp.where(lane == 0, number, tail))
        held = []
        for j in range(experts):
            e = turned(chip, j % chips, chips) * cores + turned(core, j // chips, cores)
            held.append([jnp.where(ids[p] == e, slots[p], -1) for p in range(2 * token_count)])
        for k in range(shards):
            first = pl.multiple_of(turned(s, k, shards) * depth, LANES)
            values = tokens_ref[:, pl.ds(first, depth)].astype(F32)
            at = k * (depth + LANES)
            for j in range(experts):
                body = jnp.zeros((padded, depth), F32)
                for p in range(2 * token_count):
                    value = jnp.broadcast_to(values[p // 2 : p // 2 + 1], (padded, depth))
                    body = jnp.where(wide_row == held[j][p], value, body)
                outs[j][:, at : at + depth] = body.astype(BF16)[:capacity]
        for j in range(experts):
            tail = jnp.zeros((padded, LANES), F32)
            for p in range(2 * token_count):
                tail = jnp.where(row == held[j][p], tails[p], tail)
            tail = tail.astype(BF16)[:capacity]
            for k in range(shards):
                at = k * (depth + LANES) + depth
                outs[j][:, at : at + LANES] = tail

    out = jax.ShapeDtypeStruct((capacity, shards * (depth + LANES)), BF16)
    return pl.pallas_call(
        kernel,
        out_shape=[out] * experts,
        in_specs=[
            pl.BlockSpec(memory_space=pltpu.SMEM),
            pl.BlockSpec(memory_space=pltpu.VMEM),
            pl.BlockSpec(memory_space=pltpu.SMEM),
            pl.BlockSpec(memory_space=pltpu.SMEM),
        ],
        out_specs=[pl.BlockSpec(memory_space=pltpu.VMEM)] * experts,
        name="place_rows",
    )(where, tokens, routes.T, mixing.T)


def gather_rows(where, blocks, depth):
    shards = len(blocks)
    group = blocks[0].shape[0]
    count = shards * group

    def kernel(where_ref, *refs):
        total = None
        row = lax.broadcasted_iota(jnp.int32, (count, group), 0)
        column = lax.broadcasted_iota(jnp.int32, (count, group), 1)
        for k in range(shards):
            at = turned(where_ref[1], shards - k, shards) * group
            moved = (row == column + at).astype(F32).astype(BF16)
            value = jnp.dot(moved, refs[k][...], preferred_element_type=F32)
            total = value if total is None else total + value
        total = total.astype(BF16)
        refs[shards][...] = total[:, :depth]
        refs[shards + 1][...] = total[:, depth:]

    return pl.pallas_call(
        kernel,
        out_shape=[
            jax.ShapeDtypeStruct((count, depth), BF16),
            jax.ShapeDtypeStruct((count, LANES), BF16),
        ],
        in_specs=[pl.BlockSpec(memory_space=pltpu.SMEM)]
        + [pl.BlockSpec(memory_space=pltpu.VMEM)] * shards,
        out_specs=[pl.BlockSpec(memory_space=pltpu.VMEM)] * 2,
        name="gather_rows",
    )(where, *blocks)


def column_pieces(where, table, rows, gate_weight, up_weight, shards, first, pieces, cuts, halves):
    count, depth = rows.shape
    width = gate_weight.shape[2] // shards
    block = width // cuts
    chunk = block if block <= 256 else next(c for c in (256, LANES) if block % c == 0)
    part = count // max(halves, 1)

    def kernel(where_ref, table_ref, rows_ref, gate_ref, up_ref, *outs):
        held = rows_ref[...]
        for at in range(0, block, chunk):
            for side, ref in enumerate((gate_ref, up_ref)):
                value = jnp.dot(held, ref[0, :, at : at + chunk], preferred_element_type=F32)
                value = value.astype(BF16)
                if not halves:
                    outs[side][0, :, at : at + chunk] = value
                for h in range(halves):
                    outs[side * halves + h][:, at : at + chunk] = value[h * part : (h + 1) * part]

    def weight_map(side):
        def index(i, j, where_ref, table_ref):
            return 0, 0, table_ref[(where_ref[1] * 2 + side) * shards + first + i] * cuts + j

        return index

    if halves:
        out_shape = [jax.ShapeDtypeStruct((part, width), BF16)] * (2 * halves)
        out_spec = pl.BlockSpec((part, block), lambda i, j, *_: (0, j))
    else:
        out_shape = [jax.ShapeDtypeStruct((pieces, count, width), BF16)] * 2
        out_spec = pl.BlockSpec((1, count, block), lambda i, j, *_: (i, 0, j))
    return pl.pallas_call(
        kernel,
        out_shape=out_shape,
        grid_spec=pltpu.PrefetchScalarGridSpec(
            num_scalar_prefetch=2,
            grid=(pieces, cuts),
            in_specs=[
                pl.BlockSpec((count, depth), lambda i, j, *_: (0, 0)),
                pl.BlockSpec((1, depth, block), weight_map(0)),
                pl.BlockSpec((1, depth, block), weight_map(1)),
            ],
            out_specs=[out_spec] * len(out_shape),
        ),
        compiler_params=pltpu.CompilerParams(vmem_limit_bytes=VMEM_LIMIT),
        cost_estimate=pl.CostEstimate(
            flops=4 * pieces * count * depth * width,
            bytes_accessed=4 * pieces * depth * width,
            transcendentals=0,
        ),
        name="column_pieces",
    )(where, table, rows, gate_weight, up_weight)


def plain_pieces(where, table, rows, gate_weight, up_weight, shards):
    width = gate_weight.shape[2] // shards
    both = []
    for side, weight in enumerate((gate_weight, up_weight)):
        value = jnp.dot(rows, weight[0], preferred_element_type=F32).astype(BF16)
        at = table.reshape(shards, 2, shards)[where[1], side] * width
        both.append([lax.dynamic_slice_in_dim(value, at[t], width, 1) for t in range(shards)])
    return both


def turn_columns(where, x, cores, chips):
    rows, total = x.shape[1:]
    block = total // (cores * chips)

    def index(k):
        def place(i, where_ref):
            b = where_ref[0]
            chip = turned(lax.div(b, jnp.int32(cores)), i, chips)
            return 0, 0, chip * cores + turned(lax.rem(b, jnp.int32(cores)), k, cores)

        return place

    def kernel(where_ref, *refs):
        for k in range(cores):
            refs[cores + k][...] = refs[k][...]

    return pl.pallas_call(
        kernel,
        out_shape=[jax.ShapeDtypeStruct((chips, rows, block), x.dtype)] * cores,
        grid_spec=pltpu.PrefetchScalarGridSpec(
            num_scalar_prefetch=1,
            grid=(chips,),
            in_specs=[pl.BlockSpec((1, rows, block), index(k)) for k in range(cores)],
            out_specs=[pl.BlockSpec((1, rows, block), lambda i, *_: (i, 0, 0))] * cores,
        ),
        cost_estimate=pl.CostEstimate(flops=0, bytes_accessed=4 * rows * total, transcendentals=0),
        name="turn_columns",
    )(where, *([x] * cores))


def hidden_rows(where, gate_in, up_in, gate_own, up_own, tails, base, total, shards, token_count):
    count, slice_width = gate_own.shape
    halves = len(gate_in)
    part = count // halves
    chunk = next(c for c in (256, LANES, slice_width) if slice_width % c == 0)

    def kernel(*refs):
        where_ref, refs = refs[0], refs[1:]
        gates, ups = refs[:halves], refs[halves : 2 * halves]
        gate_own_ref, up_own_ref, tail_ref, base_ref, out_ref = refs[2 * halves :]
        tail = tail_ref[...].astype(F32)
        number, weight = tail[:, 0:1], tail[:, 1:2] + tail[:, 2:3]
        shard = base_ref[...][:, 1:2] - where_ref[1].astype(F32)
        shard = jnp.where(shard < 0, shard + shards, shard)
        target = base_ref[...][:, 0:1] + shard * token_count + number
        target = jnp.where(number > 0, target, -1.0).astype(jnp.int32)
        spread = target == lax.broadcasted_iota(jnp.int32, (count, total), 1)
        spread = spread.astype(F32).astype(BF16)
        for at in range(0, slice_width, chunk):
            cut = slice(at, at + chunk)
            pieces = []
            for h in range(halves):
                line = slice(h * part, (h + 1) * part)
                gate = gates[h][:, cut].astype(F32) + gate_own_ref[line, cut].astype(F32)
                upper = ups[h][:, cut].astype(F32) + up_own_ref[line, cut].astype(F32)
                value = gate / (1.0 + jnp.exp(-gate)) * upper * weight[line]
                pieces.append(value.astype(BF16))
            hidden = jnp.concatenate(pieces, axis=0) if halves > 1 else pieces[0]
            out_ref[:, cut] = lax.dot_general(
                spread, hidden, (((0,), (0,)), ((), ())), preferred_element_type=F32
            ).astype(BF16)

    return pl.pallas_call(
        kernel,
        out_shape=jax.ShapeDtypeStruct((total, slice_width), BF16),
        cost_estimate=pl.CostEstimate(
            flops=2 * total * slice_width * count,
            bytes_accessed=8 * count * slice_width,
            transcendentals=count * slice_width,
        ),
        in_specs=[pl.BlockSpec(memory_space=pltpu.SMEM)]
        + [pl.BlockSpec(memory_space=pltpu.VMEM)] * (2 * halves + 4),
        out_specs=pl.BlockSpec(memory_space=pltpu.VMEM),
        compiler_params=pltpu.CompilerParams(vmem_limit_bytes=VMEM_LIMIT),
        name="hidden_rows",
    )(where, *gate_in, *up_in, gate_own, up_own, tails, base)


def down_half(hidden, down_weight, cores, half, halves):
    total, slice_width = hidden.shape
    width = down_weight.shape[2] // halves
    kept = total // cores
    block = 512 if width % 512 == 0 else width
    steps = width // block

    def kernel(hidden_ref, down_ref, *outs):
        value = jnp.dot(hidden_ref[...], down_ref[0], preferred_element_type=F32)
        outs[0][...] = value[:kept]
        for k in range(1, cores):
            outs[k][...] = value[k * kept : (k + 1) * kept].astype(BF16)

    shapes = [jax.ShapeDtypeStruct((kept, width), F32 if k == 0 else BF16) for k in range(cores)]
    return pl.pallas_call(
        kernel,
        out_shape=shapes,
        grid=(steps,),
        in_specs=[
            pl.BlockSpec((total, slice_width), lambda j: (0, 0)),
            pl.BlockSpec((1, slice_width, block), lambda j: (0, 0, half * steps + j)),
        ],
        out_specs=[pl.BlockSpec((kept, block), lambda j: (0, j))] * cores,
        compiler_params=pltpu.CompilerParams(vmem_limit_bytes=VMEM_LIMIT),
        cost_estimate=pl.CostEstimate(
            flops=2 * total * slice_width * width,
            bytes_accessed=2 * slice_width * width,
            transcendentals=0,
        ),
        name="down_half",
    )(hidden, down_weight)


def branch_target(size, cores, core_step, chip_step):
    chips = size // cores
    return [
        (i, (i // cores + chip_step) % chips * cores + (i + core_step) % cores)
        for i in range(size)
    ]


def shard_target(size, step):
    return [(i, (i + step) % size) for i in range(size)]


def local(order, cores, tokens, routes, mixing, gate_weight, up_weight, down_weight, key_value):
    experts = lax.axis_size("branch")
    shards = lax.axis_size("shard")
    chips = experts // cores
    token_count, width = tokens.shape
    capacity = max(2, (2 * token_count + experts - 1) // experts + 1)
    depth = gate_weight.shape[1]
    slice_width = down_weight.shape[1]
    group = experts * capacity
    count = shards * group
    halves = 2 if count % 32 == 0 and shards <= 8 else 1
    part = count // halves
    where = jnp.stack([lax.axis_index("branch"), lax.axis_index("shard")]).astype(jnp.int32)

    place = np.argsort(np.asarray(order))
    table = np.zeros((shards, 2, shards), np.int32)
    for s in range(shards):
        for t in range(shards):
            table[s, 0, t] = order[(place[s] - 1 - t) % shards]
            table[s, 1, t] = order[(place[s] + 1 + t) % shards]
    table = jnp.asarray(table.reshape(-1))
    forth = [(order[i], order[(i + 1) % shards]) for i in range(shards)]
    back = [(b, a) for a, b in forth]
    base = np.zeros((count, LANES), np.float32)
    for i in range(count):
        j = i % group // capacity
        core, chip = -(j // chips) % cores, -(j % chips) % chips
        base[i, 0] = (core * chips + chip) * shards * token_count - 1
        base[i, 1] = i // group
    base = jnp.asarray(base)

    cells = place_rows(where, tokens, routes, mixing, experts, cores, capacity, shards)
    cells, where, table, base = lax.optimization_barrier((cells, where, table, base))
    blocks = [cells[0]]
    for j in range(1, experts):
        target = branch_target(experts, cores, j // chips, j % chips)
        blocks.append(lax.ppermute(cells[j], "branch", target))
    kv = turn_columns(where, key_value, cores, chips)
    blocks, kv = lax.optimization_barrier((blocks, kv))
    blocks = jnp.concatenate(blocks, axis=0)
    cuts = jnp.split(blocks, shards, axis=1)
    for k in range(1, shards):
        cuts[k] = lax.ppermute(cuts[k], "shard", shard_target(shards, k))
    rows, tails = gather_rows(where, cuts, depth)
    kv_core = [
        lax.ppermute(kv[k], "branch", branch_target(experts, cores, k, 0))
        for k in range(1, cores)
    ]

    if slice_width % LANES == 0:
        cuts = 2 if slice_width % (2 * LANES) == 0 else 1
        one = column_pieces(
            where, table, rows, gate_weight, up_weight, shards, 0, 1, cuts, halves
        )
        gate_sum, up_sum = list(one[:halves]), list(one[halves:])
        gates, ups = column_pieces(
            where, table, rows, gate_weight, up_weight, shards, 1, shards - 1, 1, 0
        )
    else:
        gates, ups = plain_pieces(where, table, rows, gate_weight, up_weight, shards)
        gate_sum, up_sum = jnp.split(gates.pop(0), halves), jnp.split(ups.pop(0), halves)

    def added(arrived, own, h):
        own = own[h * part : (h + 1) * part]
        return (arrived.astype(F32) + own.astype(F32)).astype(BF16)

    for t in range(1, shards):
        for h in range(halves):
            gate_sum[h] = lax.ppermute(gate_sum[h], "shard", forth)
            up_sum[h] = lax.ppermute(up_sum[h], "shard", back)
        if t == min(2, shards - 1):
            gate_sum, kv_core = lax.optimization_barrier((gate_sum, kv_core))
            kv_sum = kv[0].astype(F32) + sum(x.astype(F32) for x in kv_core)
            kv_chip = [
                lax.ppermute(
                    kv_sum[k].astype(BF16), "branch", branch_target(experts, cores, 0, k)
                )
                for k in range(1, chips)
            ]
        if t == min(5, shards - 1):
            gate_sum, kv_chip = lax.optimization_barrier((gate_sum, kv_chip))
            kv_sum = kv_sum[0] + sum(x.astype(F32) for x in kv_chip)
            merged_kv = (kv_sum / experts).astype(BF16)
            gate_sum, merged_kv = lax.optimization_barrier((gate_sum, merged_kv))
        if t < shards - 1:
            for h in range(halves):
                gate_sum[h] = added(gate_sum[h], gates[t - 1], h)
                up_sum[h] = added(up_sum[h], ups[t - 1], h)

    total = experts * shards * token_count
    hidden = hidden_rows(
        where, gate_sum, up_sum, gates[shards - 2], ups[shards - 2], tails, base, total,
        shards, token_count,
    )
    mixed = []
    for half in range(2):
        outputs = down_half(hidden, down_weight, cores, half, 2)
        held = outputs[0].reshape(chips, shards * token_count, width // 2)
        for k in range(1, cores):
            sent = lax.ppermute(outputs[k], "branch", branch_target(experts, cores, k, 0))
            held = held + sent.astype(F32).reshape(held.shape)
        one = held[0]
        for k in range(1, chips):
            sent = lax.ppermute(
                held[k].astype(BF16), "branch", branch_target(experts, cores, 0, k)
            )
            one = one + sent.astype(F32)
        mixed.append(one)
    mixed = jnp.concatenate(mixed, axis=1).reshape(shards, token_count, width)
    mixed_out = mixed[0]
    for k in range(1, shards):
        sent = lax.ppermute(mixed[k].astype(BF16), "shard", shard_target(shards, k))
        mixed_out = mixed_out + sent.astype(F32)
    return mixed_out.astype(BF16), merged_kv


def solution(mesh):
    grid = mesh.devices
    order = ring_order(list(grid[0, :]))
    cores = core_count(list(grid[:, 0]))
    return jax.shard_map(
        functools.partial(local, order, cores),
        mesh=mesh,
        in_specs=(
            P(("branch", "shard"), None),
            P(("branch", "shard"), None),
            P(("branch", "shard"), None),
            P("branch", "shard", None),
            P("branch", "shard", None),
            P("branch", "shard", None),
            P("branch", "shard", None),
        ),
        out_specs=(P(("branch", "shard"), None), P("shard", "branch")),
        check_vma=False,
    )
```

```python
import functools

import jax
import jax.numpy as jnp
import numpy as np
from jax import lax
from jax.experimental import pallas as pl
from jax.experimental.pallas import tpu as pltpu
from jax.sharding import PartitionSpec as P

F32 = jnp.float32
BF16 = jnp.bfloat16
LANES = 128
VMEM_LIMIT = 24 * 1024 * 1024
PIECES_LIMIT = 48 * 1024 * 1024


def ring_order(devices):
    places = [getattr(d, "coords", None) for d in devices]
    count = len(places)
    if any(p is None for p in places):
        return list(range(count))
    at = {(p[2], p[0]): i for i, p in enumerate(places)}
    zs, xs = sorted({k[0] for k in at}), sorted({k[1] for k in at})
    if len(at) != count or len(zs) * len(xs) != count or len(xs) < 2 or len(zs) % 2:
        return list(range(count))
    order = [at[(z, xs[0])] for z in zs]
    for i, z in enumerate(reversed(zs)):
        line = xs[1:] if i % 2 == 0 else list(reversed(xs[1:]))
        order += [at[(z, x)] for x in line]
    return order


def core_count(devices):
    places = [getattr(d, "coords", None) for d in devices]
    if any(p is None for p in places):
        return 1
    same = [tuple(p) == tuple(places[0]) for p in places]
    cores = sum(same)
    return cores if all(same[:cores]) and len(places) % cores == 0 else 1


def turned(index, step, count):
    return lax.rem(index + step, jnp.int32(count))


def place_rows(tokens, routes, mixing, experts, capacity, shards):
    token_count, width = tokens.shape
    depth = width // shards
    padded = -(-capacity // 8) * 8

    def kernel(tokens_ref, routes_ref, mixing_ref, out_ref):
        ids = [routes_ref[p % 2, p // 2] for p in range(2 * token_count)]
        slots = []
        for p in range(2 * token_count):
            slot = jnp.int32(0)
            for q in range(p):
                slot = slot + jnp.where(ids[q] == ids[p], 1, 0)
            slots.append(slot)
        row = lax.broadcasted_iota(jnp.int32, (padded, LANES), 0)
        lane = lax.broadcasted_iota(jnp.int32, (padded, LANES), 1)
        wide_row = lax.broadcasted_iota(jnp.int32, (padded, width), 0)
        values = tokens_ref[...].astype(F32)
        tails = []
        for p in range(2 * token_count):
            weight = jnp.full((padded, LANES), mixing_ref[p % 2, p // 2], F32)
            high = weight.astype(BF16).astype(F32)
            number = jnp.full((padded, LANES), float(p // 2 + 1), F32)
            tail = jnp.where(lane == 1, high, jnp.where(lane == 2, weight - high, 0.0))
            tails.append(jnp.where(lane == 0, number, tail))
        for e in range(experts):
            tail = jnp.zeros((padded, LANES), F32)
            body = jnp.zeros((padded, width), F32)
            for p in range(2 * token_count):
                slot = jnp.where(ids[p] == e, slots[p], -1)
                value = jnp.broadcast_to(values[p // 2 : p // 2 + 1], (padded, width))
                tail = jnp.where(row == slot, tails[p], tail)
                body = jnp.where(wide_row == slot, value, body)
            body, tail = body.astype(BF16)[:capacity], tail.astype(BF16)[:capacity]
            for s in range(shards):
                out_ref[e * shards + s, :, :depth] = body[:, s * depth : (s + 1) * depth]
                out_ref[e * shards + s, :, depth:] = tail

    return pl.pallas_call(
        kernel,
        out_shape=jax.ShapeDtypeStruct((experts * shards, capacity, depth + LANES), BF16),
        in_specs=[
            pl.BlockSpec(memory_space=pltpu.VMEM),
            pl.BlockSpec(memory_space=pltpu.SMEM),
            pl.BlockSpec(memory_space=pltpu.SMEM),
        ],
        out_specs=pl.BlockSpec(memory_space=pltpu.VMEM),
        name="place_rows",
    )(tokens, routes.T, mixing.T)


def column_pieces(where, table, rows, gate_weight, up_weight, shards, first, pieces, cuts):
    count, depth = rows.shape
    width = gate_weight.shape[2] // shards
    block = width // cuts

    def kernel(where_ref, table_ref, rows_ref, *refs):
        weights, outs = refs[: 2 * pieces], refs[2 * pieces :]
        for ref, out in zip(weights, outs):
            value = jnp.dot(rows_ref[...], ref[0], preferred_element_type=F32)
            out[...] = value.astype(BF16)

    def weight_map(side, i):
        def index(j, where_ref, table_ref):
            return 0, 0, table_ref[(where_ref[1] * 2 + side) * shards + first + i] * cuts + j

        return pl.BlockSpec((1, depth, block), index)

    both = [(side, i) for side in range(2) for i in range(pieces)]
    out = pl.pallas_call(
        kernel,
        out_shape=[jax.ShapeDtypeStruct((count, width), BF16)] * len(both),
        grid_spec=pltpu.PrefetchScalarGridSpec(
            num_scalar_prefetch=2,
            grid=(cuts,),
            in_specs=[pl.BlockSpec((count, depth), lambda j, *_: (0, 0))]
            + [weight_map(side, i) for side, i in both],
            out_specs=[pl.BlockSpec((count, block), lambda j, *_: (0, j))] * len(both),
        ),
        compiler_params=pltpu.CompilerParams(vmem_limit_bytes=PIECES_LIMIT),
        cost_estimate=pl.CostEstimate(
            flops=4 * pieces * count * depth * width,
            bytes_accessed=4 * pieces * depth * width,
            transcendentals=0,
        ),
        name="column_pieces",
    )(where, table, rows, *([gate_weight] * pieces + [up_weight] * pieces))
    return out[:pieces], out[pieces:]


def plain_pieces(where, table, rows, gate_weight, up_weight, shards):
    width = gate_weight.shape[2] // shards
    both = []
    for side, weight in enumerate((gate_weight, up_weight)):
        value = jnp.dot(rows, weight[0], preferred_element_type=F32).astype(BF16)
        at = table.reshape(shards, 2, shards)[where[1], side] * width
        both.append([lax.dynamic_slice_in_dim(value, at[t], width, 1) for t in range(shards)])
    return both


def turn_columns(where, x, cores, chips):
    rows, total = x.shape[1:]
    block = total // (cores * chips)

    def index(k):
        def place(i, where_ref):
            b = where_ref[0]
            chip = turned(lax.div(b, jnp.int32(cores)), i, chips)
            return 0, 0, chip * cores + turned(lax.rem(b, jnp.int32(cores)), k, cores)

        return place

    def kernel(where_ref, *refs):
        for k in range(cores):
            refs[cores + k][...] = refs[k][...]

    return pl.pallas_call(
        kernel,
        out_shape=[jax.ShapeDtypeStruct((chips, rows, block), x.dtype)] * cores,
        grid_spec=pltpu.PrefetchScalarGridSpec(
            num_scalar_prefetch=1,
            grid=(chips,),
            in_specs=[pl.BlockSpec((1, rows, block), index(k)) for k in range(cores)],
            out_specs=[pl.BlockSpec((1, rows, block), lambda i, *_: (i, 0, 0))] * cores,
        ),
        cost_estimate=pl.CostEstimate(flops=0, bytes_accessed=4 * rows * total, transcendentals=0),
        name="turn_columns",
    )(where, *([x] * cores))


def hidden_rows(where, gate_in, up_in, gate_own, up_own, tails, origin, sizes):
    experts, shards, cores, token_count = sizes
    chips = experts // cores
    total = experts * shards * token_count
    count, slice_width = gate_own.shape
    chunk = next(c for c in (256, LANES, slice_width) if slice_width % c == 0)

    def kernel(where_ref, gate_ref, up_ref, gate_own_ref, up_own_ref, tail_ref, origin_ref, out_ref):
        b = where_ref[0]
        tail = tail_ref[...].astype(F32)
        place = origin_ref[...]
        number, weight = tail[:, 0:1], tail[:, 1:2] + tail[:, 2:3]
        chip = place[:, 0:1] - lax.div(b, jnp.int32(cores)).astype(F32)
        core = place[:, 1:2] - lax.rem(b, jnp.int32(cores)).astype(F32)
        chip = jnp.where(chip < 0, chip + chips, chip)
        core = jnp.where(core < 0, core + cores, core)
        target = (core * chips + chip) * (shards * token_count) + place[:, 2:3] + number - 1.0
        target = jnp.where(number > 0, target, -1.0).astype(jnp.int32)
        spread = target == lax.broadcasted_iota(jnp.int32, (count, total), 1)
        spread = spread.astype(F32).astype(BF16)
        for at in range(0, slice_width, chunk):
            cut = slice(at, at + chunk)
            gate = gate_ref[:, cut].astype(F32) + gate_own_ref[:, cut].astype(F32)
            upper = up_ref[:, cut].astype(F32) + up_own_ref[:, cut].astype(F32)
            hidden = (gate / (1.0 + jnp.exp(-gate)) * upper * weight).astype(BF16)
            out_ref[:, cut] = lax.dot_general(
                spread, hidden, (((0,), (0,)), ((), ())), preferred_element_type=F32
            ).astype(BF16)

    return pl.pallas_call(
        kernel,
        out_shape=jax.ShapeDtypeStruct((total, slice_width), BF16),
        in_specs=[pl.BlockSpec(memory_space=pltpu.SMEM)]
        + [pl.BlockSpec(memory_space=pltpu.VMEM)] * 6,
        out_specs=pl.BlockSpec(memory_space=pltpu.VMEM),
        cost_estimate=pl.CostEstimate(
            flops=2 * total * slice_width * count,
            bytes_accessed=8 * count * slice_width,
            transcendentals=count * slice_width,
        ),
        compiler_params=pltpu.CompilerParams(vmem_limit_bytes=VMEM_LIMIT),
        name="hidden_rows",
    )(where, gate_in, up_in, gate_own, up_own, tails, origin)


def hold(where, x, parts):
    rows = x.shape[1] // parts

    def kernel(where_ref, in_ref, out_ref, sems):
        copies = [
            pltpu.make_async_copy(
                in_ref.at[:, pl.ds(i * rows, rows)], out_ref.at[:, pl.ds(i * rows, rows)], sems.at[i]
            )
            for i in range(parts)
        ]
        for copy in copies:
            copy.start()
        for copy in copies:
            copy.wait()

    return pl.pallas_call(
        kernel,
        out_shape=jax.ShapeDtypeStruct(x.shape, x.dtype),
        in_specs=[pl.BlockSpec(memory_space=pltpu.SMEM), pl.BlockSpec(memory_space=pl.ANY)],
        out_specs=pl.BlockSpec(memory_space=pl.ANY),
        scratch_shapes=[pltpu.SemaphoreType.DMA((parts,))],
        cost_estimate=pl.CostEstimate(
            flops=0, bytes_accessed=2 * x.size * x.dtype.itemsize, transcendentals=0
        ),
        name="hold",
    )(where, x)


def branch_target(size, cores, core_step, chip_step):
    chips = size // cores
    return [
        (i, (i // cores + chip_step) % chips * cores + (i + core_step) % cores)
        for i in range(size)
    ]


def local(order, cores, tokens, routes, mixing, gate_weight, up_weight, down_weight, key_value):
    experts = lax.axis_size("branch")
    shards = lax.axis_size("shard")
    chips = experts // cores
    token_count, width = tokens.shape
    capacity = max(2, (2 * token_count + experts - 1) // experts + 1)
    depth = gate_weight.shape[1]
    slice_width = down_weight.shape[1]
    count = experts * shards * capacity
    kept = chips * shards * token_count
    sizes = (experts, shards, cores, token_count)
    where = jnp.stack([lax.axis_index("branch"), lax.axis_index("shard")]).astype(jnp.int32)

    place = np.argsort(np.asarray(order))
    table = np.zeros((shards, 2, shards), np.int32)
    for s in range(shards):
        for t in range(shards):
            table[s, 0, t] = order[(place[s] - 1 - t) % shards]
            table[s, 1, t] = order[(place[s] + 1 + t) % shards]
    table = jnp.asarray(table.reshape(-1))
    forth = [(order[i], order[(i + 1) % shards]) for i in range(shards)]
    back = [(b, a) for a, b in forth]
    source = np.arange(count) // capacity
    origin = np.zeros((count, LANES), np.float32)
    origin[:, 0] = source // shards // cores
    origin[:, 1] = source // shards % cores
    origin[:, 2] = source % shards * token_count
    origin = jnp.asarray(origin)

    cells = place_rows(tokens, routes, mixing, experts, capacity, shards)
    cells, where, table, origin = lax.optimization_barrier((cells, where, table, origin))
    cells = lax.all_to_all(cells, ("branch", "shard"), split_axis=0, concat_axis=0, tiled=True)
    cells = cells.reshape(count, depth + LANES)
    rows, tails = cells[:, :depth], cells[:, depth:]

    sliced = slice_width % LANES == 0
    if sliced:
        cuts = 2 if slice_width % (2 * LANES) == 0 else 1
        gates, ups = column_pieces(where, table, rows, gate_weight, up_weight, shards, 0, 1, cuts)
    else:
        gates, ups = plain_pieces(where, table, rows, gate_weight, up_weight, shards)
    gate_sum, up_sum = gates[0], ups[0]
    last = shards - 1
    for t in range(1, shards):
        now, gate_sum, up_sum = lax.optimization_barrier((where, gate_sum, up_sum))
        gate_in = lax.ppermute(gate_sum, "shard", forth)
        up_in = lax.ppermute(up_sum, "shard", back)
        if sliced and len(gates) < shards:
            more = column_pieces(
                now, table, rows, gate_weight, up_weight, shards, len(gates),
                min(2, shards - len(gates)), 1,
            )
            gates, ups = gates + more[0], ups + more[1]
            gate_in, up_in, gates, ups = lax.optimization_barrier((gate_in, up_in, gates, ups))
        if t == min(4, last):
            kv = turn_columns(now, key_value, cores, chips)
            kv_core = [
                lax.ppermute(kv[k], "branch", branch_target(experts, cores, k, 0))
                for k in range(1, cores)
            ]
            gate_in, kv = lax.optimization_barrier((gate_in, kv))
        if t == min(5, last):
            gate_in, kv_core = lax.optimization_barrier((gate_in, kv_core))
            kv_sum = kv[0].astype(F32) + sum(x.astype(F32) for x in kv_core)
            kv_chip = [
                lax.ppermute(
                    kv_sum[k].astype(BF16), "branch", branch_target(experts, cores, 0, k)
                )
                for k in range(1, chips)
            ]
        if t == min(6, last):
            down_here = hold(now, down_weight, 8 if slice_width % LANES == 0 else 1)
            gate_in, down_here = lax.optimization_barrier((gate_in, down_here))
        if t == last:
            gate_in, kv_chip = lax.optimization_barrier((gate_in, kv_chip))
            kv_sum = kv_sum[0] + sum(x.astype(F32) for x in kv_chip)
            merged_kv = (kv_sum / experts).astype(BF16)
            gate_in, merged_kv = lax.optimization_barrier((gate_in, merged_kv))
        else:
            gate_sum = (gate_in.astype(F32) + gates[t].astype(F32)).astype(BF16)
            up_sum = (up_in.astype(F32) + ups[t].astype(F32)).astype(BF16)

    hidden = hidden_rows(where, gate_in, up_in, gates[last], ups[last], tails, origin, sizes)
    sent = []
    for k in range(1, cores):
        part = jnp.dot(
            hidden[k * kept : (k + 1) * kept], down_here[0], preferred_element_type=F32
        ).astype(BF16)
        sent.append(lax.ppermute(part, "branch", branch_target(experts, cores, k, 0)))
    mixed = jnp.dot(hidden[:kept], down_here[0], preferred_element_type=F32)
    mixed, sent = lax.optimization_barrier((mixed, sent))
    mixed = mixed + sum(x.astype(F32) for x in sent)
    mixed = mixed.reshape(chips, shards * token_count, width)
    total = mixed[0]
    for k in range(1, chips):
        part = lax.ppermute(mixed[k].astype(BF16), "branch", branch_target(experts, cores, 0, k))
        total = total + part.astype(F32)
    total = total.astype(BF16).reshape(shards, token_count, width)
    total = lax.all_to_all(total, "shard", split_axis=0, concat_axis=0, tiled=True)
    return jnp.sum(total.astype(F32), axis=0).astype(BF16), merged_kv


def solution(mesh):
    grid = mesh.devices
    order = ring_order(list(grid[0, :]))
    cores = core_count(list(grid[:, 0]))
    return jax.shard_map(
        functools.partial(local, order, cores),
        mesh=mesh,
        in_specs=(
            P(("branch", "shard"), None),
            P(("branch", "shard"), None),
            P(("branch", "shard"), None),
            P("branch", "shard", None),
            P("branch", "shard", None),
            P("branch", "shard", None),
            P("branch", "shard", None),
        ),
        out_specs=(P(("branch", "shard"), None), P("shard", "branch")),
        check_vma=False,
    )
```

```python
import functools

import jax
import jax.numpy as jnp
import numpy as np
from jax import lax
from jax.experimental import pallas as pl
from jax.experimental.pallas import tpu as pltpu
from jax.sharding import PartitionSpec as P

F32 = jnp.float32
BF16 = jnp.bfloat16
LANES = 128
VMEM_LIMIT = 48 * 1024 * 1024


def ring_order(devices):
    places = [getattr(d, "coords", None) for d in devices]
    count = len(places)
    if any(p is None for p in places):
        return list(range(count))
    at = {(p[2], p[0]): i for i, p in enumerate(places)}
    zs, xs = sorted({k[0] for k in at}), sorted({k[1] for k in at})
    if len(at) != count or len(zs) * len(xs) != count or len(xs) < 2 or len(zs) % 2:
        return list(range(count))
    order = [at[(z, xs[0])] for z in zs]
    for i, z in enumerate(reversed(zs)):
        line = xs[1:] if i % 2 == 0 else list(reversed(xs[1:]))
        order += [at[(z, x)] for x in line]
    return order


def core_count(devices):
    places = [getattr(d, "coords", None) for d in devices]
    if any(p is None for p in places):
        return 1
    same = [tuple(p) == tuple(places[0]) for p in places]
    cores = sum(same)
    return cores if all(same[:cores]) and len(places) % cores == 0 else 1


def turned(index, step, count):
    return lax.rem(index + step, jnp.int32(count))


def place_rows(tokens, routes, mixing, experts, capacity, shards):
    token_count, width = tokens.shape
    depth = width // shards
    padded = -(-capacity // 8) * 8

    def kernel(tokens_ref, routes_ref, mixing_ref, out_ref):
        ids = [routes_ref[p % 2, p // 2] for p in range(2 * token_count)]
        slots = []
        for p in range(2 * token_count):
            slot = jnp.int32(0)
            for q in range(p):
                slot = slot + jnp.where(ids[q] == ids[p], 1, 0)
            slots.append(slot)
        row = lax.broadcasted_iota(jnp.int32, (padded, LANES), 0)
        lane = lax.broadcasted_iota(jnp.int32, (padded, LANES), 1)
        wide_row = lax.broadcasted_iota(jnp.int32, (padded, width), 0)
        values = tokens_ref[...].astype(F32)
        tails = []
        for p in range(2 * token_count):
            weight = jnp.full((padded, LANES), mixing_ref[p % 2, p // 2], F32)
            high = weight.astype(BF16).astype(F32)
            number = jnp.full((padded, LANES), float(p // 2 + 1), F32)
            tail = jnp.where(lane == 1, high, jnp.where(lane == 2, weight - high, 0.0))
            tails.append(jnp.where(lane == 0, number, tail))
        for e in range(experts):
            tail = jnp.zeros((padded, LANES), F32)
            body = jnp.zeros((padded, width), F32)
            for p in range(2 * token_count):
                slot = jnp.where(ids[p] == e, slots[p], -1)
                value = jnp.broadcast_to(values[p // 2 : p // 2 + 1], (padded, width))
                tail = jnp.where(row == slot, tails[p], tail)
                body = jnp.where(wide_row == slot, value, body)
            body, tail = body.astype(BF16)[:capacity], tail.astype(BF16)[:capacity]
            for s in range(shards):
                out_ref[e * shards + s, :, :depth] = body[:, s * depth : (s + 1) * depth]
                out_ref[e * shards + s, :, depth:] = tail

    return pl.pallas_call(
        kernel,
        out_shape=jax.ShapeDtypeStruct((experts * shards, capacity, depth + LANES), BF16),
        in_specs=[
            pl.BlockSpec(memory_space=pltpu.VMEM),
            pl.BlockSpec(memory_space=pltpu.SMEM),
            pl.BlockSpec(memory_space=pltpu.SMEM),
        ],
        out_specs=pl.BlockSpec(memory_space=pltpu.VMEM),
        name="place_rows",
    )(tokens, routes.T, mixing.T)


def row_parts(rows):
    return 4 if rows % 64 == 0 else 1


def column_piece(where, table, rows, gate_weight, up_weight, shards, step, cuts):
    count, depth = rows.shape
    width = gate_weight.shape[2] // shards
    block = width // cuts
    parts = row_parts(depth)

    def kernel(where_ref, table_ref, rows_ref, *refs):
        for side in range(2):
            weight = [ref[0] for ref in refs[side * parts : (side + 1) * parts]]
            weight = jnp.concatenate(weight, axis=0) if parts > 1 else weight[0]
            value = jnp.dot(rows_ref[...], weight, preferred_element_type=F32)
            refs[2 * parts + side][...] = value.astype(BF16)

    def weight_block(side, part):
        def index(j, where_ref, table_ref):
            return 0, part, table_ref[(where_ref[1] * 2 + side) * shards + step] * cuts + j

        return pl.BlockSpec((1, depth // parts, block), index)

    return pl.pallas_call(
        kernel,
        out_shape=[jax.ShapeDtypeStruct((count, width), BF16)] * 2,
        grid_spec=pltpu.PrefetchScalarGridSpec(
            num_scalar_prefetch=2,
            grid=(cuts,),
            in_specs=[pl.BlockSpec((count, depth), lambda j, *_: (0, 0))]
            + [weight_block(side, part) for side in range(2) for part in range(parts)],
            out_specs=[pl.BlockSpec((count, block), lambda j, *_: (0, j))] * 2,
        ),
        compiler_params=pltpu.CompilerParams(vmem_limit_bytes=VMEM_LIMIT),
        cost_estimate=pl.CostEstimate(
            flops=4 * count * depth * width, bytes_accessed=4 * depth * width, transcendentals=0
        ),
        name="column_piece",
    )(where, table, rows, *([gate_weight] * parts + [up_weight] * parts))


def plain_pieces(where, table, rows, gate_weight, up_weight, shards):
    width = gate_weight.shape[2] // shards
    both = []
    for side, weight in enumerate((gate_weight, up_weight)):
        value = jnp.dot(rows, weight[0], preferred_element_type=F32).astype(BF16)
        at = table.reshape(shards, 2, shards)[where[1], side] * width
        both.append([lax.dynamic_slice_in_dim(value, at[t], width, 1) for t in range(shards)])
    return both


def turn_columns(where, x, cores, chips):
    rows, total = x.shape[1:]
    block = total // (cores * chips)

    def index(k):
        def place(i, where_ref):
            b = where_ref[0]
            chip = turned(lax.div(b, jnp.int32(cores)), i, chips)
            return 0, 0, chip * cores + turned(lax.rem(b, jnp.int32(cores)), k, cores)

        return place

    def kernel(where_ref, *refs):
        for k in range(cores):
            refs[cores + k][...] = refs[k][...]

    return pl.pallas_call(
        kernel,
        out_shape=[jax.ShapeDtypeStruct((chips, rows, block), x.dtype)] * cores,
        grid_spec=pltpu.PrefetchScalarGridSpec(
            num_scalar_prefetch=1,
            grid=(chips,),
            in_specs=[pl.BlockSpec((1, rows, block), index(k)) for k in range(cores)],
            out_specs=[pl.BlockSpec((1, rows, block), lambda i, *_: (i, 0, 0))] * cores,
        ),
        cost_estimate=pl.CostEstimate(flops=0, bytes_accessed=4 * rows * total, transcendentals=0),
        name="turn_columns",
    )(where, *([x] * cores))


def expert_outputs(where, gate_in, up_in, gate_own, up_own, tails, origin, down_weight, sizes):
    experts, shards, cores, token_count = sizes
    chips = experts // cores
    count, slice_width = gate_in.shape
    width = down_weight.shape[2]
    total = experts * shards * token_count
    kept = total // cores
    block = 512 if width % 512 == 0 else width
    parts = row_parts(slice_width)
    chunk = next(c for c in (256, 128, slice_width) if slice_width % c == 0)

    def kernel(where_ref, gate_ref, up_ref, gate_own_ref, up_own_ref, tail_ref, origin_ref, *rest):
        hidden_ref = rest[-1]
        weights, outs = rest[:parts], rest[parts:-1]

        @pl.when(pl.program_id(0) == 0)
        def _():
            b = where_ref[0]
            tail = tail_ref[...].astype(F32)
            place = origin_ref[...]
            number, weight = tail[:, 0:1], tail[:, 1:2] + tail[:, 2:3]
            chip = place[:, 0:1] - lax.div(b, jnp.int32(cores)).astype(F32)
            core = place[:, 1:2] - lax.rem(b, jnp.int32(cores)).astype(F32)
            chip = jnp.where(chip < 0, chip + chips, chip)
            core = jnp.where(core < 0, core + cores, core)
            target = (core * chips + chip) * (shards * token_count) + place[:, 2:3] + number - 1.0
            target = jnp.where(number > 0, target, -1.0).astype(jnp.int32)
            spread = target == lax.broadcasted_iota(jnp.int32, (count, total), 1)
            spread = spread.astype(F32).astype(BF16)
            for at in range(0, slice_width, chunk):
                cut = slice(at, at + chunk)
                gate = gate_ref[:, cut].astype(F32) + gate_own_ref[:, cut].astype(F32)
                upper = up_ref[:, cut].astype(F32) + up_own_ref[:, cut].astype(F32)
                hidden = (gate / (1.0 + jnp.exp(-gate)) * upper * weight).astype(BF16)
                hidden_ref[:, cut] = lax.dot_general(
                    spread, hidden, (((0,), (0,)), ((), ())), preferred_element_type=F32
                ).astype(BF16)

        weight = [ref[0] for ref in weights]
        weight = jnp.concatenate(weight, axis=0) if parts > 1 else weight[0]
        value = jnp.dot(hidden_ref[...], weight, preferred_element_type=F32)
        outs[0][...] = value[:kept]
        if cores > 1:
            outs[1][...] = value[kept:].astype(BF16)

    def weight_block(part):
        return pl.BlockSpec((1, slice_width // parts, block), lambda j, *_: (0, part, j))

    whole = pl.BlockSpec((count, slice_width), lambda j, *_: (0, 0))
    lanes = pl.BlockSpec((count, LANES), lambda j, *_: (0, 0))
    shapes = [jax.ShapeDtypeStruct((kept, width), F32)]
    specs = [pl.BlockSpec((kept, block), lambda j, *_: (0, j))]
    if cores > 1:
        shapes.append(jax.ShapeDtypeStruct((total - kept, width), BF16))
        specs.append(pl.BlockSpec((total - kept, block), lambda j, *_: (0, j)))
    return pl.pallas_call(
        kernel,
        out_shape=shapes,
        grid_spec=pltpu.PrefetchScalarGridSpec(
            num_scalar_prefetch=1,
            grid=(width // block,),
            in_specs=[
                whole, whole, whole, whole, lanes, lanes,
            ]
            + [weight_block(part) for part in range(parts)],
            out_specs=specs,
            scratch_shapes=[pltpu.VMEM((total, slice_width), BF16)],
        ),
        compiler_params=pltpu.CompilerParams(vmem_limit_bytes=VMEM_LIMIT),
        cost_estimate=pl.CostEstimate(
            flops=2 * total * slice_width * width,
            bytes_accessed=2 * slice_width * width,
            transcendentals=count * slice_width,
        ),
        name="expert_outputs",
    )(where, gate_in, up_in, gate_own, up_own, tails, origin, *([down_weight] * parts))


def branch_target(size, cores, core_step, chip_step):
    chips = size // cores
    return [
        (i, (i // cores + chip_step) % chips * cores + (i + core_step) % cores)
        for i in range(size)
    ]


def local(order, cores, tokens, routes, mixing, gate_weight, up_weight, down_weight, key_value):
    experts = lax.axis_size("branch")
    shards = lax.axis_size("shard")
    chips = experts // cores
    token_count, width = tokens.shape
    capacity = max(2, (2 * token_count + experts - 1) // experts + 1)
    depth = gate_weight.shape[1]
    slice_width = down_weight.shape[1]
    count = experts * shards * capacity
    sizes = (experts, shards, cores, token_count)
    where = jnp.stack([lax.axis_index("branch"), lax.axis_index("shard")]).astype(jnp.int32)

    place = np.argsort(np.asarray(order))
    table = np.zeros((shards, 2, shards), np.int32)
    for s in range(shards):
        for t in range(shards):
            table[s, 0, t] = order[(place[s] - 1 - t) % shards]
            table[s, 1, t] = order[(place[s] + 1 + t) % shards]
    table = jnp.asarray(table.reshape(-1))
    forth = [(order[i], order[(i + 1) % shards]) for i in range(shards)]
    back = [(b, a) for a, b in forth]
    source = np.arange(count) // capacity
    origin = np.zeros((count, LANES), np.float32)
    origin[:, 0] = source // shards // cores
    origin[:, 1] = source // shards % cores
    origin[:, 2] = source % shards * token_count
    origin = jnp.asarray(origin)

    cells = place_rows(tokens, routes, mixing, experts, capacity, shards)
    cells, where, table, origin = lax.optimization_barrier((cells, where, table, origin))
    cells = lax.all_to_all(cells, ("branch", "shard"), split_axis=0, concat_axis=0, tiled=True)
    cells = cells.reshape(count, depth + LANES)
    rows, tails = cells[:, :depth], cells[:, depth:]

    sliced = slice_width % LANES == 0
    if sliced:
        cuts = 2 if slice_width % (2 * LANES) == 0 else 1
        one = column_piece(where, table, rows, gate_weight, up_weight, shards, 0, cuts)
        gates, ups = [one[0]], [one[1]]
    else:
        gates, ups = plain_pieces(where, table, rows, gate_weight, up_weight, shards)
    gate_sum, up_sum = gates[0], ups[0]
    last = shards - 1
    for t in range(1, shards):
        now, gate_sum, up_sum = lax.optimization_barrier((where, gate_sum, up_sum))
        gate_in = lax.ppermute(gate_sum, "shard", forth)
        up_in = lax.ppermute(up_sum, "shard", back)
        if sliced:
            one = column_piece(now, table, rows, gate_weight, up_weight, shards, t, cuts)
            gate_in, up_in, one = lax.optimization_barrier((gate_in, up_in, one))
            gates.append(one[0])
            ups.append(one[1])
        if t == 1:
            kv = turn_columns(now, key_value, cores, chips)
            kv_core = [
                lax.ppermute(kv[k], "branch", branch_target(experts, cores, k, 0))
                for k in range(1, cores)
            ]
            gate_in, kv = lax.optimization_barrier((gate_in, kv))
        if t == min(2, last):
            gate_in, kv_core = lax.optimization_barrier((gate_in, kv_core))
            kv_sum = kv[0].astype(F32) + sum(x.astype(F32) for x in kv_core)
            kv_chip = [
                lax.ppermute(
                    kv_sum[k].astype(BF16), "branch", branch_target(experts, cores, 0, k)
                )
                for k in range(1, chips)
            ]
        if t == min(5, last):
            gate_in, kv_chip = lax.optimization_barrier((gate_in, kv_chip))
            kv_sum = kv_sum[0] + sum(x.astype(F32) for x in kv_chip)
            merged_kv = (kv_sum / experts).astype(BF16)
            gate_in, merged_kv = lax.optimization_barrier((gate_in, merged_kv))
        if t < last:
            gate_sum = (gate_in.astype(F32) + gates[t].astype(F32)).astype(BF16)
            up_sum = (up_in.astype(F32) + ups[t].astype(F32)).astype(BF16)

    outputs = expert_outputs(
        where, gate_in, up_in, gates[last], ups[last], tails, origin, down_weight, sizes
    )
    mixed = outputs[0].reshape(chips, shards * token_count, width)
    for k in range(1, cores):
        sent = outputs[1].reshape(cores - 1, chips, shards * token_count, width)[k - 1]
        part = lax.ppermute(sent, "branch", branch_target(experts, cores, k, 0))
        mixed = mixed + part.astype(F32)
    total = mixed[0]
    for k in range(1, chips):
        part = lax.ppermute(mixed[k].astype(BF16), "branch", branch_target(experts, cores, 0, k))
        total = total + part.astype(F32)
    total = total.astype(BF16).reshape(shards, token_count, width)
    total = lax.all_to_all(total, "shard", split_axis=0, concat_axis=0, tiled=True)
    return jnp.sum(total.astype(F32), axis=0).astype(BF16), merged_kv


def solution(mesh):
    grid = mesh.devices
    order = ring_order(list(grid[0, :]))
    cores = core_count(list(grid[:, 0]))
    return jax.shard_map(
        functools.partial(local, order, cores),
        mesh=mesh,
        in_specs=(
            P(("branch", "shard"), None),
            P(("branch", "shard"), None),
            P(("branch", "shard"), None),
            P("branch", "shard", None),
            P("branch", "shard", None),
            P("branch", "shard", None),
            P("branch", "shard", None),
        ),
        out_specs=(P(("branch", "shard"), None), P("shard", "branch")),
        check_vma=False,
    )
```

```python
import functools

import jax
import jax.numpy as jnp
import numpy as np
from jax import lax
from jax.experimental import pallas as pl
from jax.experimental.pallas import tpu as pltpu
from jax.sharding import PartitionSpec as P

F32 = jnp.float32
BF16 = jnp.bfloat16
LANES = 128
VMEM_LIMIT = 48 * 1024 * 1024


def ring_order(devices):
    places = [getattr(d, "coords", None) for d in devices]
    count = len(places)
    if any(p is None for p in places):
        return list(range(count))
    at = {(p[2], p[0]): i for i, p in enumerate(places)}
    zs, xs = sorted({k[0] for k in at}), sorted({k[1] for k in at})
    if len(at) != count or len(zs) * len(xs) != count or len(xs) < 2 or len(zs) % 2:
        return list(range(count))
    order = [at[(z, xs[0])] for z in zs]
    for i, z in enumerate(reversed(zs)):
        line = xs[1:] if i % 2 == 0 else list(reversed(xs[1:]))
        order += [at[(z, x)] for x in line]
    return order


def grid_columns(devices):
    places = [getattr(d, "coords", None) for d in devices]
    if any(p is None for p in places):
        return 1
    columns = len({p[0] for p in places})
    line = sorted(range(len(places)), key=lambda i: (places[i][2], places[i][0]))
    whole = len({(p[2], p[0]) for p in places}) == len(places)
    return columns if whole and line == list(range(len(places))) and len(places) % columns == 0 else 1


def core_count(devices):
    places = [getattr(d, "coords", None) for d in devices]
    if any(p is None for p in places):
        return 1
    same = [tuple(p) == tuple(places[0]) for p in places]
    cores = sum(same)
    return cores if all(same[:cores]) and len(places) % cores == 0 else 1


def turned(index, step, count):
    return lax.rem(index + step, jnp.int32(count))


def place_rows(tokens, routes, mixing, experts, capacity, shards):
    token_count, width = tokens.shape
    depth = width // shards
    padded = -(-capacity // 8) * 8

    def kernel(tokens_ref, routes_ref, mixing_ref, out_ref):
        ids = [routes_ref[p % 2, p // 2] for p in range(2 * token_count)]
        slots = []
        for p in range(2 * token_count):
            slot = jnp.int32(0)
            for q in range(p):
                slot = slot + jnp.where(ids[q] == ids[p], 1, 0)
            slots.append(slot)
        row = lax.broadcasted_iota(jnp.int32, (padded, LANES), 0)
        lane = lax.broadcasted_iota(jnp.int32, (padded, LANES), 1)
        wide_row = lax.broadcasted_iota(jnp.int32, (padded, width), 0)
        values = tokens_ref[...].astype(F32)
        tails = []
        for p in range(2 * token_count):
            weight = jnp.full((padded, LANES), mixing_ref[p % 2, p // 2], F32)
            high = weight.astype(BF16).astype(F32)
            number = jnp.full((padded, LANES), float(p // 2 + 1), F32)
            tail = jnp.where(lane == 1, high, jnp.where(lane == 2, weight - high, 0.0))
            tails.append(jnp.where(lane == 0, number, tail))
        for e in range(experts):
            tail = jnp.zeros((padded, LANES), F32)
            body = jnp.zeros((padded, width), F32)
            for p in range(2 * token_count):
                slot = jnp.where(ids[p] == e, slots[p], -1)
                value = jnp.broadcast_to(values[p // 2 : p // 2 + 1], (padded, width))
                tail = jnp.where(row == slot, tails[p], tail)
                body = jnp.where(wide_row == slot, value, body)
            body, tail = body.astype(BF16)[:capacity], tail.astype(BF16)[:capacity]
            for s in range(shards):
                out_ref[e * shards + s, :, :depth] = body[:, s * depth : (s + 1) * depth]
                out_ref[e * shards + s, :, depth:] = tail

    return pl.pallas_call(
        kernel,
        out_shape=jax.ShapeDtypeStruct((experts * shards, capacity, depth + LANES), BF16),
        in_specs=[
            pl.BlockSpec(memory_space=pltpu.VMEM),
            pl.BlockSpec(memory_space=pltpu.SMEM),
            pl.BlockSpec(memory_space=pltpu.SMEM),
        ],
        out_specs=pl.BlockSpec(memory_space=pltpu.VMEM),
        name="place_rows",
    )(tokens, routes.T, mixing.T)


def row_parts(rows):
    return 4 if rows % 64 == 0 else 1


def column_piece(where, table, rows, gate_weight, up_weight, shards, step, cuts):
    count, depth = rows.shape
    width = gate_weight.shape[2] // shards
    block = width // cuts
    parts = row_parts(depth)

    def kernel(where_ref, table_ref, rows_ref, *refs):
        for side in range(2):
            weight = [ref[0] for ref in refs[side * parts : (side + 1) * parts]]
            weight = jnp.concatenate(weight, axis=0) if parts > 1 else weight[0]
            value = jnp.dot(rows_ref[...], weight, preferred_element_type=F32)
            refs[2 * parts + side][...] = value.astype(BF16)

    def weight_block(side, part):
        def index(j, where_ref, table_ref):
            return 0, part, table_ref[(where_ref[1] * 2 + side) * shards + step] * cuts + j

        return pl.BlockSpec((1, depth // parts, block), index)

    return pl.pallas_call(
        kernel,
        out_shape=[jax.ShapeDtypeStruct((count, width), BF16)] * 2,
        grid_spec=pltpu.PrefetchScalarGridSpec(
            num_scalar_prefetch=2,
            grid=(cuts,),
            in_specs=[pl.BlockSpec((count, depth), lambda j, *_: (0, 0))]
            + [weight_block(side, part) for side in range(2) for part in range(parts)],
            out_specs=[pl.BlockSpec((count, block), lambda j, *_: (0, j))] * 2,
        ),
        compiler_params=pltpu.CompilerParams(vmem_limit_bytes=VMEM_LIMIT),
        cost_estimate=pl.CostEstimate(
            flops=4 * count * depth * width, bytes_accessed=4 * depth * width, transcendentals=0
        ),
        name="column_piece",
    )(where, table, rows, *([gate_weight] * parts + [up_weight] * parts))


def plain_pieces(where, table, rows, gate_weight, up_weight, shards):
    width = gate_weight.shape[2] // shards
    both = []
    for side, weight in enumerate((gate_weight, up_weight)):
        value = jnp.dot(rows, weight[0], preferred_element_type=F32).astype(BF16)
        at = table.reshape(shards, 2, shards)[where[1], side] * width
        both.append([lax.dynamic_slice_in_dim(value, at[t], width, 1) for t in range(shards)])
    return both


def turn_columns(where, x, cores, chips):
    rows, total = x.shape[1:]
    block = total // (cores * chips)

    def index(k):
        def place(i, where_ref):
            b = where_ref[0]
            chip = turned(lax.div(b, jnp.int32(cores)), i, chips)
            return 0, 0, chip * cores + turned(lax.rem(b, jnp.int32(cores)), k, cores)

        return place

    def kernel(where_ref, *refs):
        for k in range(cores):
            refs[cores + k][...] = refs[k][...]

    return pl.pallas_call(
        kernel,
        out_shape=[jax.ShapeDtypeStruct((chips, rows, block), x.dtype)] * cores,
        grid_spec=pltpu.PrefetchScalarGridSpec(
            num_scalar_prefetch=1,
            grid=(chips,),
            in_specs=[pl.BlockSpec((1, rows, block), index(k)) for k in range(cores)],
            out_specs=[pl.BlockSpec((1, rows, block), lambda i, *_: (i, 0, 0))] * cores,
        ),
        cost_estimate=pl.CostEstimate(flops=0, bytes_accessed=4 * rows * total, transcendentals=0),
        name="turn_columns",
    )(where, *([x] * cores))


def expert_outputs(where, gate_in, up_in, gate_own, up_own, tails, origin, down_weight, sizes):
    experts, shards, cores, columns, token_count = sizes
    chips, lines = experts // cores, shards // columns
    count, slice_width = gate_in.shape
    width = down_weight.shape[2]
    total = experts * shards * token_count
    kept = total // cores
    block = 256 if slice_width % 256 == 0 else slice_width
    steps = slice_width // block
    chunk = 512 if width % 512 == 0 else width

    def kernel(where_ref, gate_ref, up_ref, gate_own_ref, up_own_ref, tail_ref, origin_ref, down_ref, *rest):
        outs, spread_ref, sum_ref = rest[:-2], rest[-2], rest[-1]
        step = pl.program_id(0)
        tail = tail_ref[...].astype(F32)
        weight = tail[:, 1:2] + tail[:, 2:3]

        @pl.when(step == 0)
        def _():
            b, s = where_ref[0], where_ref[1]
            mine = (
                lax.rem(b, jnp.int32(cores)), lax.div(b, jnp.int32(cores)),
                lax.rem(s, jnp.int32(columns)), lax.div(s, jnp.int32(columns)),
            )
            number, place = tail[:, 0:1], origin_ref[...]
            target = jnp.zeros((count, 1), F32)
            for i, size in enumerate((cores, chips, columns, lines)):
                away = place[:, i : i + 1] - mine[i].astype(F32)
                target = target * size + jnp.where(away < 0, away + size, away)
            target = target * token_count + number - 1.0
            target = jnp.where(number > 0, target, -1.0).astype(jnp.int32)
            spread = target == lax.broadcasted_iota(jnp.int32, (count, total), 1)
            spread_ref[...] = spread.astype(F32).astype(BF16)

        gate = gate_ref[...].astype(F32) + gate_own_ref[...].astype(F32)
        upper = up_ref[...].astype(F32) + up_own_ref[...].astype(F32)
        hidden = (gate / (1.0 + jnp.exp(-gate)) * upper * weight).astype(BF16)
        hidden = lax.dot_general(
            spread_ref[...], hidden, (((0,), (0,)), ((), ())), preferred_element_type=F32
        ).astype(BF16)

        def add(first):
            for at in range(0, width, chunk):
                cut = slice(at, at + chunk)
                value = jnp.dot(hidden, down_ref[0, :, cut], preferred_element_type=F32)
                if first:
                    outs[0][:, cut] = value[:kept]
                    if cores > 1:
                        sum_ref[:, cut] = value[kept:]
                else:
                    outs[0][:, cut] += value[:kept]
                    if cores > 1:
                        sum_ref[:, cut] += value[kept:]

        pl.when(step == 0)(lambda: add(True))
        pl.when(step > 0)(lambda: add(False))
        if cores > 1:

            @pl.when(step == steps - 1)
            def _():
                for at in range(0, width, chunk):
                    cut = slice(at, at + chunk)
                    outs[1][:, cut] = sum_ref[:, cut].astype(BF16)

    part = pl.BlockSpec((count, block), lambda j, *_: (0, j))
    lanes = pl.BlockSpec((count, LANES), lambda j, *_: (0, 0))
    shapes = [jax.ShapeDtypeStruct((kept, width), F32)]
    specs = [pl.BlockSpec((kept, width), lambda j, *_: (0, 0))]
    if cores > 1:
        shapes.append(jax.ShapeDtypeStruct((total - kept, width), BF16))
        specs.append(pl.BlockSpec((total - kept, width), lambda j, *_: (0, 0)))
    return pl.pallas_call(
        kernel,
        out_shape=shapes,
        grid_spec=pltpu.PrefetchScalarGridSpec(
            num_scalar_prefetch=1,
            grid=(steps,),
            in_specs=[
                part, part, part, part, lanes, lanes,
                pl.BlockSpec((1, block, width), lambda j, *_: (0, j, 0)),
            ],
            out_specs=specs,
            scratch_shapes=[
                pltpu.VMEM((count, total), BF16),
                pltpu.VMEM((max(total - kept, 8), width), F32),
            ],
        ),
        compiler_params=pltpu.CompilerParams(vmem_limit_bytes=VMEM_LIMIT),
        cost_estimate=pl.CostEstimate(
            flops=2 * total * slice_width * width,
            bytes_accessed=2 * slice_width * width,
            transcendentals=count * slice_width,
        ),
        name="expert_outputs",
    )(where, gate_in, up_in, gate_own, up_own, tails, origin, down_weight)


def branch_target(size, cores, core_step, chip_step):
    chips = size // cores
    return [
        (i, (i // cores + chip_step) % chips * cores + (i + core_step) % cores)
        for i in range(size)
    ]


def shard_target(size, columns, x_step, z_step):
    lines = size // columns
    return [
        (i, (i // columns + z_step) % lines * columns + (i + x_step) % columns)
        for i in range(size)
    ]


def direct_sum(x, axis_name, target):
    total = x[0]
    for k in range(1, x.shape[0]):
        total = total + lax.ppermute(x[k].astype(BF16), axis_name, target(k)).astype(F32)
    return total


def local(order, cores, columns, tokens, routes, mixing, gate_weight, up_weight, down_weight, key_value):
    experts = lax.axis_size("branch")
    shards = lax.axis_size("shard")
    chips = experts // cores
    token_count, width = tokens.shape
    capacity = max(2, (2 * token_count + experts - 1) // experts + 1)
    depth = gate_weight.shape[1]
    slice_width = down_weight.shape[1]
    count = experts * shards * capacity
    lines = shards // columns
    sizes = (experts, shards, cores, columns, token_count)
    where = jnp.stack([lax.axis_index("branch"), lax.axis_index("shard")]).astype(jnp.int32)

    place = np.argsort(np.asarray(order))
    table = np.zeros((shards, 2, shards), np.int32)
    for s in range(shards):
        for t in range(shards):
            table[s, 0, t] = order[(place[s] - 1 - t) % shards]
            table[s, 1, t] = order[(place[s] + 1 + t) % shards]
    table = jnp.asarray(table.reshape(-1))
    forth = [(order[i], order[(i + 1) % shards]) for i in range(shards)]
    back = [(b, a) for a, b in forth]
    source = np.arange(count) // capacity
    origin = np.zeros((count, LANES), np.float32)
    origin[:, 0] = source // shards % cores
    origin[:, 1] = source // shards // cores
    origin[:, 2] = source % shards % columns
    origin[:, 3] = source % shards // columns
    origin = jnp.asarray(origin)

    cells = place_rows(tokens, routes, mixing, experts, capacity, shards)
    cells, where, table, origin = lax.optimization_barrier((cells, where, table, origin))
    cells = lax.all_to_all(cells, ("branch", "shard"), split_axis=0, concat_axis=0, tiled=True)
    cells = cells.reshape(count, depth + LANES)
    rows, tails = cells[:, :depth], cells[:, depth:]

    sliced = slice_width % LANES == 0
    if sliced:
        cuts = 2 if slice_width % (2 * LANES) == 0 else 1
        one = column_piece(where, table, rows, gate_weight, up_weight, shards, 0, cuts)
        gates, ups = [one[0]], [one[1]]
    else:
        gates, ups = plain_pieces(where, table, rows, gate_weight, up_weight, shards)
    gate_sum, up_sum = gates[0], ups[0]
    last = shards - 1
    for t in range(1, shards):
        now, gate_sum = lax.optimization_barrier((where, gate_sum))
        gate_in = lax.ppermute(gate_sum, "shard", forth)
        up_in = lax.ppermute(up_sum, "shard", back)
        if sliced:
            one = column_piece(now, table, rows, gate_weight, up_weight, shards, t, cuts)
            gates.append(one[0])
            ups.append(one[1])
        if t == 1:
            kv = turn_columns(now, key_value, cores, chips)
            kv_core = [
                lax.ppermute(kv[k], "branch", branch_target(experts, cores, k, 0))
                for k in range(1, cores)
            ]
            gate_in, kv = lax.optimization_barrier((gate_in, kv))
        if t == min(2, last):
            gate_in, kv_core = lax.optimization_barrier((gate_in, kv_core))
            kv_sum = kv[0].astype(F32) + sum(x.astype(F32) for x in kv_core)
            kv_chip = [
                lax.ppermute(
                    kv_sum[k].astype(BF16), "branch", branch_target(experts, cores, 0, k)
                )
                for k in range(1, chips)
            ]
        if t == min(5, last):
            gate_in, kv_chip = lax.optimization_barrier((gate_in, kv_chip))
            kv_sum = kv_sum[0] + sum(x.astype(F32) for x in kv_chip)
            merged_kv = (kv_sum / experts).astype(BF16)
            gate_in, merged_kv = lax.optimization_barrier((gate_in, merged_kv))
        if t < last:
            gate_sum = (gate_in.astype(F32) + gates[t].astype(F32)).astype(BF16)
            up_sum = (up_in.astype(F32) + ups[t].astype(F32)).astype(BF16)

    outputs = expert_outputs(
        where, gate_in, up_in, gates[last], ups[last], tails, origin, down_weight, sizes
    )
    mixed = outputs[0]
    for k in range(1, cores):
        sent = outputs[1].reshape(cores - 1, -1, width)[k - 1]
        part = lax.ppermute(sent, "branch", branch_target(experts, cores, k, 0))
        mixed = mixed + part.astype(F32)

    def over_chips(x):
        return direct_sum(x, "branch", lambda k: branch_target(experts, cores, 0, k))

    def over_columns(x):
        return direct_sum(x, "shard", lambda k: shard_target(shards, columns, k, 0))

    def over_lines(x):
        return direct_sum(x, "shard", lambda k: shard_target(shards, columns, 0, k))

    mixed = mixed.reshape(chips, columns, lines * token_count, width)
    left = over_chips(mixed[..., : width // 2])
    right = over_columns(mixed[..., width // 2 :].swapaxes(0, 1))
    left, right = over_columns(left), over_chips(right)
    mixed = jnp.concatenate([left, right], axis=1).reshape(lines, token_count, width)
    return over_lines(mixed).astype(BF16), merged_kv


def solution(mesh):
    grid = mesh.devices
    order = ring_order(list(grid[0, :]))
    cores = core_count(list(grid[:, 0]))
    columns = grid_columns(list(grid[0, :]))
    return jax.shard_map(
        functools.partial(local, order, cores, columns),
        mesh=mesh,
        in_specs=(
            P(("branch", "shard"), None),
            P(("branch", "shard"), None),
            P(("branch", "shard"), None),
            P("branch", "shard", None),
            P("branch", "shard", None),
            P("branch", "shard", None),
            P("branch", "shard", None),
        ),
        out_specs=(P(("branch", "shard"), None), P("shard", "branch")),
        check_vma=False,
    )
```

```python
import functools

import jax
import jax.numpy as jnp
import numpy as np
from jax import lax
from jax.experimental import pallas as pl
from jax.experimental.pallas import tpu as pltpu
from jax.sharding import PartitionSpec as P

F32 = jnp.float32
BF16 = jnp.bfloat16
LANES = 128
VMEM_LIMIT = 40 * 1024 * 1024
HIDDEN_LIMIT = 24 * 1024 * 1024


def ring_order(devices):
    places = [getattr(d, "coords", None) for d in devices]
    count = len(places)
    if any(p is None for p in places):
        return list(range(count))
    at = {(p[2], p[0]): i for i, p in enumerate(places)}
    zs, xs = sorted({k[0] for k in at}), sorted({k[1] for k in at})
    if len(at) != count or len(zs) * len(xs) != count or len(xs) < 2 or len(zs) % 2:
        return list(range(count))
    order = [at[(z, xs[0])] for z in zs]
    for i, z in enumerate(reversed(zs)):
        line = xs[1:] if i % 2 == 0 else list(reversed(xs[1:]))
        order += [at[(z, x)] for x in line]
    return order


def grid_columns(devices):
    places = [getattr(d, "coords", None) for d in devices]
    if any(p is None for p in places):
        return 1
    columns = len({p[0] for p in places})
    line = sorted(range(len(places)), key=lambda i: (places[i][2], places[i][0]))
    whole = len({(p[2], p[0]) for p in places}) == len(places)
    return columns if whole and line == list(range(len(places))) and len(places) % columns == 0 else 1


def core_count(devices):
    places = [getattr(d, "coords", None) for d in devices]
    if any(p is None for p in places):
        return 1
    same = [tuple(p) == tuple(places[0]) for p in places]
    cores = sum(same)
    return cores if all(same[:cores]) and len(places) % cores == 0 else 1


def turned(index, step, count):
    return lax.rem(index + step, jnp.int32(count))


def place_rows(tokens, routes, mixing, experts, capacity, shards):
    token_count, width = tokens.shape
    depth = width // shards
    padded = -(-capacity // 8) * 8

    def kernel(tokens_ref, routes_ref, mixing_ref, out_ref):
        ids = [routes_ref[p % 2, p // 2] for p in range(2 * token_count)]
        slots = []
        for p in range(2 * token_count):
            slot = jnp.int32(0)
            for q in range(p):
                slot = slot + jnp.where(ids[q] == ids[p], 1, 0)
            slots.append(slot)
        row = lax.broadcasted_iota(jnp.int32, (padded, LANES), 0)
        lane = lax.broadcasted_iota(jnp.int32, (padded, LANES), 1)
        wide_row = lax.broadcasted_iota(jnp.int32, (padded, width), 0)
        values = tokens_ref[...].astype(F32)
        tails = []
        for p in range(2 * token_count):
            weight = jnp.full((padded, LANES), mixing_ref[p % 2, p // 2], F32)
            high = weight.astype(BF16).astype(F32)
            number = jnp.full((padded, LANES), float(p // 2 + 1), F32)
            tail = jnp.where(lane == 1, high, jnp.where(lane == 2, weight - high, 0.0))
            tails.append(jnp.where(lane == 0, number, tail))
        for e in range(experts):
            tail = jnp.zeros((padded, LANES), F32)
            body = jnp.zeros((padded, width), F32)
            for p in range(2 * token_count):
                slot = jnp.where(ids[p] == e, slots[p], -1)
                value = jnp.broadcast_to(values[p // 2 : p // 2 + 1], (padded, width))
                tail = jnp.where(row == slot, tails[p], tail)
                body = jnp.where(wide_row == slot, value, body)
            body, tail = body.astype(BF16)[:capacity], tail.astype(BF16)[:capacity]
            for s in range(shards):
                out_ref[e * shards + s, :, :depth] = body[:, s * depth : (s + 1) * depth]
                out_ref[e * shards + s, :, depth:] = tail

    return pl.pallas_call(
        kernel,
        out_shape=jax.ShapeDtypeStruct((experts * shards, capacity, depth + LANES), BF16),
        in_specs=[
            pl.BlockSpec(memory_space=pltpu.VMEM),
            pl.BlockSpec(memory_space=pltpu.SMEM),
            pl.BlockSpec(memory_space=pltpu.SMEM),
        ],
        out_specs=pl.BlockSpec(memory_space=pltpu.VMEM),
        name="place_rows",
    )(tokens, routes.T, mixing.T)


def column_pieces(where, table, rows, gate_weight, up_weight, shards, first, pieces, cuts):
    count, depth = rows.shape
    width = gate_weight.shape[2] // shards
    block = width // cuts

    def kernel(where_ref, table_ref, rows_ref, *refs):
        weights, outs = refs[: 2 * pieces], refs[2 * pieces :]
        for ref, out in zip(weights, outs):
            value = jnp.dot(rows_ref[...], ref[0], preferred_element_type=F32)
            out[...] = value.astype(BF16)

    def weight_map(side, i):
        def index(j, where_ref, table_ref):
            return 0, 0, table_ref[(where_ref[1] * 2 + side) * shards + first + i] * cuts + j

        return pl.BlockSpec((1, depth, block), index)

    both = [(side, i) for side in range(2) for i in range(pieces)]
    out = pl.pallas_call(
        kernel,
        out_shape=[jax.ShapeDtypeStruct((count, width), BF16)] * len(both),
        grid_spec=pltpu.PrefetchScalarGridSpec(
            num_scalar_prefetch=2,
            grid=(cuts,),
            in_specs=[pl.BlockSpec((count, depth), lambda j, *_: (0, 0))]
            + [weight_map(side, i) for side, i in both],
            out_specs=[pl.BlockSpec((count, block), lambda j, *_: (0, j))] * len(both),
        ),
        compiler_params=pltpu.CompilerParams(vmem_limit_bytes=VMEM_LIMIT),
        cost_estimate=pl.CostEstimate(
            flops=4 * pieces * count * depth * width,
            bytes_accessed=4 * pieces * depth * width,
            transcendentals=0,
        ),
        name="column_pieces",
    )(where, table, rows, *([gate_weight] * pieces + [up_weight] * pieces))
    return out[:pieces], out[pieces:]


def plain_pieces(where, table, rows, gate_weight, up_weight, shards):
    width = gate_weight.shape[2] // shards
    both = []
    for side, weight in enumerate((gate_weight, up_weight)):
        value = jnp.dot(rows, weight[0], preferred_element_type=F32).astype(BF16)
        at = table.reshape(shards, 2, shards)[where[1], side] * width
        both.append([lax.dynamic_slice_in_dim(value, at[t], width, 1) for t in range(shards)])
    return both


def turn_columns(where, x, cores, chips):
    rows, total = x.shape[1:]
    block = total // (cores * chips)

    def index(k):
        def place(i, where_ref):
            b = where_ref[0]
            chip = turned(lax.div(b, jnp.int32(cores)), i, chips)
            return 0, 0, chip * cores + turned(lax.rem(b, jnp.int32(cores)), k, cores)

        return place

    def kernel(where_ref, *refs):
        for k in range(cores):
            refs[cores + k][...] = refs[k][...]

    return pl.pallas_call(
        kernel,
        out_shape=[jax.ShapeDtypeStruct((chips, rows, block), x.dtype)] * cores,
        grid_spec=pltpu.PrefetchScalarGridSpec(
            num_scalar_prefetch=1,
            grid=(chips,),
            in_specs=[pl.BlockSpec((1, rows, block), index(k)) for k in range(cores)],
            out_specs=[pl.BlockSpec((1, rows, block), lambda i, *_: (i, 0, 0))] * cores,
        ),
        cost_estimate=pl.CostEstimate(flops=0, bytes_accessed=4 * rows * total, transcendentals=0),
        name="turn_columns",
    )(where, *([x] * cores))


def hidden_rows(where, gate_in, up_in, gate_own, up_own, tails, origin, sizes, parts):
    experts, shards, cores, columns, token_count = sizes
    chips, lines = experts // cores, shards // columns
    total = experts * shards * token_count
    kept = total // cores
    count, slice_width = gate_own.shape
    cut_width = slice_width // parts
    chunk = next(c for c in (256, LANES, cut_width) if cut_width % c == 0)

    def kernel(where_ref, gate_ref, up_ref, gate_own_ref, up_own_ref, tail_ref, origin_ref, *outs):
        b, s = where_ref[0], where_ref[1]
        mine = (
            lax.rem(b, jnp.int32(cores)), lax.div(b, jnp.int32(cores)),
            lax.rem(s, jnp.int32(columns)), jnp.int32(0),
        )
        tail = tail_ref[...].astype(F32)
        number, weight = tail[:, 0:1], tail[:, 1:2] + tail[:, 2:3]
        place = origin_ref[...]
        target = jnp.zeros((count, 1), F32)
        for i, size in enumerate((cores, chips, columns, lines)):
            away = place[:, i : i + 1] - mine[i].astype(F32)
            target = target * size + jnp.where(away < 0, away + size, away)
        target = target * token_count + number - 1.0
        target = jnp.where(number > 0, target, -1.0).astype(jnp.int32)
        spread = target == lax.broadcasted_iota(jnp.int32, (count, total), 1)
        spread = spread.astype(F32).astype(BF16)
        for at in range(0, slice_width, chunk):
            cut = slice(at, at + chunk)
            gate = gate_ref[:, cut].astype(F32) + gate_own_ref[:, cut].astype(F32)
            upper = up_ref[:, cut].astype(F32) + up_own_ref[:, cut].astype(F32)
            hidden = (gate / (1.0 + jnp.exp(-gate)) * upper * weight).astype(BF16)
            hidden = lax.dot_general(
                spread, hidden, (((0,), (0,)), ((), ())), preferred_element_type=F32
            ).astype(BF16)
            part, to = at // cut_width, at % cut_width
            if cores > 1:
                outs[part][:, to : to + chunk] = hidden[kept:]
            outs[len(outs) - parts + part][:, to : to + chunk] = hidden[:kept]

    shapes = [jax.ShapeDtypeStruct((kept, cut_width), BF16)] * parts
    if cores > 1:
        shapes = [jax.ShapeDtypeStruct((total - kept, cut_width), BF16)] * parts + shapes
    return pl.pallas_call(
        kernel,
        out_shape=shapes,
        in_specs=[pl.BlockSpec(memory_space=pltpu.SMEM)]
        + [pl.BlockSpec(memory_space=pltpu.VMEM)] * 6,
        out_specs=[pl.BlockSpec(memory_space=pltpu.VMEM)] * len(shapes),
        cost_estimate=pl.CostEstimate(
            flops=2 * total * slice_width * count,
            bytes_accessed=8 * count * slice_width,
            transcendentals=count * slice_width,
        ),
        compiler_params=pltpu.CompilerParams(vmem_limit_bytes=HIDDEN_LIMIT),
        name="hidden_rows",
    )(where, gate_in, up_in, gate_own, up_own, tails, origin)


def down_product(hidden, weights):
    return sum(jnp.dot(h, w, preferred_element_type=F32) for h, w in zip(hidden, weights))


def branch_target(size, cores, core_step, chip_step):
    chips = size // cores
    return [
        (i, (i // cores + chip_step) % chips * cores + (i + core_step) % cores)
        for i in range(size)
    ]


def shard_target(size, columns, x_step, z_step):
    lines = size // columns
    return [
        (i, (i // columns + z_step) % lines * columns + (i + x_step) % columns)
        for i in range(size)
    ]


def direct_sum(x, axis_name, target):
    total = x[0]
    for k in range(1, x.shape[0]):
        total = total + lax.ppermute(x[k].astype(BF16), axis_name, target(k)).astype(F32)
    return total


def local(order, cores, columns, tokens, routes, mixing, gate_weight, up_weight, down_weight, key_value):
    experts = lax.axis_size("branch")
    shards = lax.axis_size("shard")
    chips = experts // cores
    token_count, width = tokens.shape
    capacity = max(2, (2 * token_count + experts - 1) // experts + 1)
    depth = gate_weight.shape[1]
    slice_width = down_weight.shape[1]
    count = experts * shards * capacity
    lines = shards // columns
    sizes = (experts, shards, cores, columns, token_count)
    where = jnp.stack([lax.axis_index("branch"), lax.axis_index("shard")]).astype(jnp.int32)

    place = np.argsort(np.asarray(order))
    table = np.zeros((shards, 2, shards), np.int32)
    for s in range(shards):
        for t in range(shards):
            table[s, 0, t] = order[(place[s] - 1 - t) % shards]
            table[s, 1, t] = order[(place[s] + 1 + t) % shards]
    table = jnp.asarray(table.reshape(-1))
    forth = [(order[i], order[(i + 1) % shards]) for i in range(shards)]
    back = [(b, a) for a, b in forth]
    source = np.arange(count) // capacity
    origin = np.zeros((count, LANES), np.float32)
    origin[:, 0] = source // shards % cores
    origin[:, 1] = source // shards // cores
    origin[:, 2] = source % shards % columns
    origin[:, 3] = source % shards // columns
    origin = jnp.asarray(origin)

    cells = place_rows(tokens, routes, mixing, experts, capacity, shards)
    cells, where, table, origin = lax.optimization_barrier((cells, where, table, origin))
    cells = lax.all_to_all(cells, ("branch", "shard"), split_axis=0, concat_axis=0, tiled=True)
    cells = cells.reshape(count, depth + LANES)
    rows, tails = cells[:, :depth], cells[:, depth:]

    sliced = slice_width % LANES == 0
    if sliced:
        cuts = 2 if slice_width % (2 * LANES) == 0 else 1
        gates, ups = column_pieces(where, table, rows, gate_weight, up_weight, shards, 0, 1, cuts)
    else:
        gates, ups = plain_pieces(where, table, rows, gate_weight, up_weight, shards)
    gate_sum, up_sum = gates[0], ups[0]
    last = shards - 1
    parts = 1
    weights = [down_weight[0]]
    for t in range(1, shards):
        now, gate_sum = lax.optimization_barrier((where, gate_sum))
        gate_in = lax.ppermute(gate_sum, "shard", forth)
        up_in = lax.ppermute(up_sum, "shard", back)
        if sliced and len(gates) < shards:
            more = column_pieces(
                now, table, rows, gate_weight, up_weight, shards, len(gates),
                1 if t == 1 else min(2, shards - len(gates)), 1,
            )
            gates, ups = gates + more[0], ups + more[1]
        if t == 1:
            kv = turn_columns(now, key_value, cores, chips)
            kv_core = [
                lax.ppermute(kv[k], "branch", branch_target(experts, cores, k, 0))
                for k in range(1, cores)
            ]
            gate_in, kv = lax.optimization_barrier((gate_in, kv))
        if t == min(2, last):
            gate_in, kv_core = lax.optimization_barrier((gate_in, kv_core))
            kv_sum = kv[0].astype(F32) + sum(x.astype(F32) for x in kv_core)
            kv_chip = [
                lax.ppermute(
                    kv_sum[k].astype(BF16), "branch", branch_target(experts, cores, 0, k)
                )
                for k in range(1, chips)
            ]
        if t == min(5, last):
            gate_in, kv_chip = lax.optimization_barrier((gate_in, kv_chip))
            kv_sum = kv_sum[0] + sum(x.astype(F32) for x in kv_chip)
            merged_kv = (kv_sum / experts).astype(BF16)
            gate_in, merged_kv = lax.optimization_barrier((gate_in, merged_kv))
        if t < last:
            gate_sum = (gate_in.astype(F32) + gates[t].astype(F32)).astype(BF16)
            up_sum = (up_in.astype(F32) + ups[t].astype(F32)).astype(BF16)

    hidden = hidden_rows(
        where, gate_in, up_in, gates[last], ups[last], tails, origin, sizes, parts
    )
    sent = []
    if cores > 1:
        others = down_product(hidden[:parts], weights).astype(BF16)
        others = others.reshape(cores - 1, -1, width)
        sent = [
            lax.ppermute(others[k - 1], "branch", branch_target(experts, cores, k, 0))
            for k in range(1, cores)
        ]
    mixed = down_product(hidden[-parts:], weights)
    mixed, sent = lax.optimization_barrier((mixed, sent))
    mixed = mixed + sum(x.astype(F32) for x in sent)

    def over_chips(x):
        return direct_sum(x, "branch", lambda k: branch_target(experts, cores, 0, k))

    def over_columns(x):
        return direct_sum(x, "shard", lambda k: shard_target(shards, columns, k, 0))

    mixed = mixed.reshape(chips, columns, lines * token_count, width)
    left = over_chips(mixed[..., : width // 2])
    right = over_columns(mixed[..., width // 2 :].swapaxes(0, 1))
    left, right = over_columns(left), over_chips(right)
    mixed = jnp.concatenate([left, right], axis=1).reshape(lines, token_count, width)
    groups = [[z * columns + x for z in range(lines)] for x in range(columns)]
    mixed = lax.all_to_all(
        mixed.astype(BF16), "shard", split_axis=0, concat_axis=0, axis_index_groups=groups, tiled=True
    )
    return jnp.sum(mixed.astype(F32), axis=0).astype(BF16), merged_kv


def solution(mesh):
    grid = mesh.devices
    order = ring_order(list(grid[0, :]))
    cores = core_count(list(grid[:, 0]))
    columns = grid_columns(list(grid[0, :]))
    return jax.shard_map(
        functools.partial(local, order, cores, columns),
        mesh=mesh,
        in_specs=(
            P(("branch", "shard"), None),
            P(("branch", "shard"), None),
            P(("branch", "shard"), None),
            P("branch", "shard", None),
            P("branch", "shard", None),
            P("branch", "shard", None),
            P("branch", "shard", None),
        ),
        out_specs=(P(("branch", "shard"), None), P("shard", "branch")),
        check_vma=False,
    )
```

```python
import functools

import jax
import jax.numpy as jnp
import numpy as np
from jax import lax
from jax.experimental import pallas as pl
from jax.experimental.pallas import tpu as pltpu
from jax.sharding import PartitionSpec as P

F32 = jnp.float32
BF16 = jnp.bfloat16
LANES = 128
VMEM_LIMIT = 40 * 1024 * 1024
HIDDEN_LIMIT = 24 * 1024 * 1024


def ring_order(devices):
    places = [getattr(d, "coords", None) for d in devices]
    count = len(places)
    if any(p is None for p in places):
        return list(range(count))
    at = {(p[2], p[0]): i for i, p in enumerate(places)}
    zs, xs = sorted({k[0] for k in at}), sorted({k[1] for k in at})
    if len(at) != count or len(zs) * len(xs) != count or len(xs) < 2 or len(zs) % 2:
        return list(range(count))
    order = [at[(z, xs[0])] for z in zs]
    for i, z in enumerate(reversed(zs)):
        line = xs[1:] if i % 2 == 0 else list(reversed(xs[1:]))
        order += [at[(z, x)] for x in line]
    return order


def core_count(devices):
    places = [getattr(d, "coords", None) for d in devices]
    if any(p is None for p in places):
        return 1
    same = [tuple(p) == tuple(places[0]) for p in places]
    cores = sum(same)
    return cores if all(same[:cores]) and len(places) % cores == 0 else 1


def turned(index, step, count):
    return lax.rem(index + step, jnp.int32(count))


def place_rows(tokens, routes, mixing, experts, capacity, shards):
    token_count, width = tokens.shape
    depth = width // shards
    padded = -(-capacity // 8) * 8

    def kernel(tokens_ref, routes_ref, mixing_ref, out_ref):
        ids = [routes_ref[p % 2, p // 2] for p in range(2 * token_count)]
        slots = []
        for p in range(2 * token_count):
            slot = jnp.int32(0)
            for q in range(p):
                slot = slot + jnp.where(ids[q] == ids[p], 1, 0)
            slots.append(slot)
        row = lax.broadcasted_iota(jnp.int32, (padded, LANES), 0)
        lane = lax.broadcasted_iota(jnp.int32, (padded, LANES), 1)
        wide_row = lax.broadcasted_iota(jnp.int32, (padded, width), 0)
        values = tokens_ref[...].astype(F32)
        tails = []
        for p in range(2 * token_count):
            weight = jnp.full((padded, LANES), mixing_ref[p % 2, p // 2], F32)
            high = weight.astype(BF16).astype(F32)
            number = jnp.full((padded, LANES), float(p // 2 + 1), F32)
            tail = jnp.where(lane == 1, high, jnp.where(lane == 2, weight - high, 0.0))
            tails.append(jnp.where(lane == 0, number, tail))
        for e in range(experts):
            tail = jnp.zeros((padded, LANES), F32)
            body = jnp.zeros((padded, width), F32)
            for p in range(2 * token_count):
                slot = jnp.where(ids[p] == e, slots[p], -1)
                value = jnp.broadcast_to(values[p // 2 : p // 2 + 1], (padded, width))
                tail = jnp.where(row == slot, tails[p], tail)
                body = jnp.where(wide_row == slot, value, body)
            body, tail = body.astype(BF16)[:capacity], tail.astype(BF16)[:capacity]
            for s in range(shards):
                out_ref[e * shards + s, :, :depth] = body[:, s * depth : (s + 1) * depth]
                out_ref[e * shards + s, :, depth:] = tail

    return pl.pallas_call(
        kernel,
        out_shape=jax.ShapeDtypeStruct((experts * shards, capacity, depth + LANES), BF16),
        in_specs=[
            pl.BlockSpec(memory_space=pltpu.VMEM),
            pl.BlockSpec(memory_space=pltpu.SMEM),
            pl.BlockSpec(memory_space=pltpu.SMEM),
        ],
        out_specs=pl.BlockSpec(memory_space=pltpu.VMEM),
        name="place_rows",
    )(tokens, routes.T, mixing.T)


def column_pieces(where, table, rows, gate_weight, up_weight, shards, first, pieces, cuts):
    count, depth = rows.shape
    width = gate_weight.shape[2] // shards
    block = width // cuts

    def kernel(where_ref, table_ref, rows_ref, *refs):
        weights, outs = refs[: 2 * pieces], refs[2 * pieces :]
        for ref, out in zip(weights, outs):
            value = jnp.dot(rows_ref[...], ref[0], preferred_element_type=F32)
            out[...] = value.astype(BF16)

    def weight_map(side, i):
        def index(j, where_ref, table_ref):
            return 0, 0, table_ref[(where_ref[1] * 2 + side) * shards + first + i] * cuts + j

        return pl.BlockSpec((1, depth, block), index)

    both = [(side, i) for side in range(2) for i in range(pieces)]
    out = pl.pallas_call(
        kernel,
        out_shape=[jax.ShapeDtypeStruct((count, width), BF16)] * len(both),
        grid_spec=pltpu.PrefetchScalarGridSpec(
            num_scalar_prefetch=2,
            grid=(cuts,),
            in_specs=[pl.BlockSpec((count, depth), lambda j, *_: (0, 0))]
            + [weight_map(side, i) for side, i in both],
            out_specs=[pl.BlockSpec((count, block), lambda j, *_: (0, j))] * len(both),
        ),
        compiler_params=pltpu.CompilerParams(vmem_limit_bytes=VMEM_LIMIT),
        cost_estimate=pl.CostEstimate(
            flops=4 * pieces * count * depth * width,
            bytes_accessed=4 * pieces * depth * width,
            transcendentals=0,
        ),
        name="column_pieces",
    )(where, table, rows, *([gate_weight] * pieces + [up_weight] * pieces))
    return out[:pieces], out[pieces:]


def plain_pieces(where, table, rows, gate_weight, up_weight, shards):
    width = gate_weight.shape[2] // shards
    both = []
    for side, weight in enumerate((gate_weight, up_weight)):
        value = jnp.dot(rows, weight[0], preferred_element_type=F32).astype(BF16)
        at = table.reshape(shards, 2, shards)[where[1], side] * width
        both.append([lax.dynamic_slice_in_dim(value, at[t], width, 1) for t in range(shards)])
    return both


def turn_columns(where, x, cores, chips):
    rows, total = x.shape[1:]
    block = total // (cores * chips)

    def index(k):
        def place(i, where_ref):
            b = where_ref[0]
            chip = turned(lax.div(b, jnp.int32(cores)), i, chips)
            return 0, 0, chip * cores + turned(lax.rem(b, jnp.int32(cores)), k, cores)

        return place

    def kernel(where_ref, *refs):
        for k in range(cores):
            refs[cores + k][...] = refs[k][...]

    return pl.pallas_call(
        kernel,
        out_shape=[jax.ShapeDtypeStruct((chips, rows, block), x.dtype)] * cores,
        grid_spec=pltpu.PrefetchScalarGridSpec(
            num_scalar_prefetch=1,
            grid=(chips,),
            in_specs=[pl.BlockSpec((1, rows, block), index(k)) for k in range(cores)],
            out_specs=[pl.BlockSpec((1, rows, block), lambda i, *_: (i, 0, 0))] * cores,
        ),
        cost_estimate=pl.CostEstimate(flops=0, bytes_accessed=4 * rows * total, transcendentals=0),
        name="turn_columns",
    )(where, *([x] * cores))


def hidden_rows(where, gate_in, up_in, gate_own, up_own, tails, origin, sizes, parts):
    experts, shards, cores, token_count = sizes
    chips = experts // cores
    total = experts * shards * token_count
    kept = total // cores
    count, slice_width = gate_own.shape
    cut_width = slice_width // parts
    chunk = next(c for c in (256, LANES, cut_width) if cut_width % c == 0)

    def kernel(where_ref, gate_ref, up_ref, gate_own_ref, up_own_ref, tail_ref, origin_ref, *outs):
        tail = tail_ref[...].astype(F32)
        number, weight = tail[:, 0:1], tail[:, 1:2] + tail[:, 2:3]
        place = origin_ref[...]
        core = place[:, 0:1] - lax.rem(where_ref[0], jnp.int32(cores)).astype(F32)
        core = jnp.where(core < 0, core + cores, core)
        target = (core * chips + place[:, 1:2]) * shards + place[:, 2:3]
        target = target * token_count + number - 1.0
        target = jnp.where(number > 0, target, -1.0).astype(jnp.int32)
        spread = target == lax.broadcasted_iota(jnp.int32, (count, total), 1)
        spread = spread.astype(F32).astype(BF16)
        for at in range(0, slice_width, chunk):
            cut = slice(at, at + chunk)
            gate = gate_ref[:, cut].astype(F32) + gate_own_ref[:, cut].astype(F32)
            upper = up_ref[:, cut].astype(F32) + up_own_ref[:, cut].astype(F32)
            hidden = (gate / (1.0 + jnp.exp(-gate)) * upper * weight).astype(BF16)
            hidden = lax.dot_general(
                spread, hidden, (((0,), (0,)), ((), ())), preferred_element_type=F32
            ).astype(BF16)
            part, to = at // cut_width, at % cut_width
            if cores > 1:
                outs[part][:, to : to + chunk] = hidden[kept:]
            outs[len(outs) - parts + part][:, to : to + chunk] = hidden[:kept]

    shapes = [jax.ShapeDtypeStruct((kept, cut_width), BF16)] * parts
    if cores > 1:
        shapes = [jax.ShapeDtypeStruct((total - kept, cut_width), BF16)] * parts + shapes
    return pl.pallas_call(
        kernel,
        out_shape=shapes,
        in_specs=[pl.BlockSpec(memory_space=pltpu.SMEM)]
        + [pl.BlockSpec(memory_space=pltpu.VMEM)] * 6,
        out_specs=[pl.BlockSpec(memory_space=pltpu.VMEM)] * len(shapes),
        cost_estimate=pl.CostEstimate(
            flops=2 * total * slice_width * count,
            bytes_accessed=8 * count * slice_width,
            transcendentals=count * slice_width,
        ),
        compiler_params=pltpu.CompilerParams(vmem_limit_bytes=HIDDEN_LIMIT),
        name="hidden_rows",
    )(where, gate_in, up_in, gate_own, up_own, tails, origin)


def down_product(hidden, weights):
    return sum(jnp.dot(h, w, preferred_element_type=F32) for h, w in zip(hidden, weights))


def branch_target(size, cores, core_step, chip_step):
    chips = size // cores
    return [
        (i, (i // cores + chip_step) % chips * cores + (i + core_step) % cores)
        for i in range(size)
    ]


def local(order, cores, tokens, routes, mixing, gate_weight, up_weight, down_weight, key_value):
    experts = lax.axis_size("branch")
    shards = lax.axis_size("shard")
    chips = experts // cores
    token_count, width = tokens.shape
    capacity = max(2, (2 * token_count + experts - 1) // experts + 1)
    depth = gate_weight.shape[1]
    slice_width = down_weight.shape[1]
    count = experts * shards * capacity
    sizes = (experts, shards, cores, token_count)
    where = jnp.stack([lax.axis_index("branch"), lax.axis_index("shard")]).astype(jnp.int32)

    place = np.argsort(np.asarray(order))
    table = np.zeros((shards, 2, shards), np.int32)
    for s in range(shards):
        for t in range(shards):
            table[s, 0, t] = order[(place[s] - 1 - t) % shards]
            table[s, 1, t] = order[(place[s] + 1 + t) % shards]
    table = jnp.asarray(table.reshape(-1))
    forth = [(order[i], order[(i + 1) % shards]) for i in range(shards)]
    back = [(b, a) for a, b in forth]
    source = np.arange(count) // capacity
    origin = np.zeros((count, LANES), np.float32)
    origin[:, 0] = source // shards % cores
    origin[:, 1] = source // shards // cores
    origin[:, 2] = source % shards
    origin = jnp.asarray(origin)

    cells = place_rows(tokens, routes, mixing, experts, capacity, shards)
    cells, where, table, origin = lax.optimization_barrier((cells, where, table, origin))
    cells = lax.all_to_all(cells, ("branch", "shard"), split_axis=0, concat_axis=0, tiled=True)
    cells = cells.reshape(count, depth + LANES)
    rows, tails = cells[:, :depth], cells[:, depth:]

    sliced = slice_width % LANES == 0
    if sliced:
        cuts = 2 if slice_width % (2 * LANES) == 0 else 1
        gates, ups = column_pieces(where, table, rows, gate_weight, up_weight, shards, 0, 1, cuts)
    else:
        gates, ups = plain_pieces(where, table, rows, gate_weight, up_weight, shards)
    gate_sum, up_sum = gates[0], ups[0]
    last = shards - 1
    parts = 1
    weights = [down_weight[0]]
    for t in range(1, shards):
        now, gate_sum = lax.optimization_barrier((where, gate_sum))
        gate_in = lax.ppermute(gate_sum, "shard", forth)
        up_in = lax.ppermute(up_sum, "shard", back)
        if sliced and len(gates) < shards:
            more = column_pieces(
                now, table, rows, gate_weight, up_weight, shards, len(gates), 1, cuts
            )
            gates, ups = gates + more[0], ups + more[1]
        if t == 1:
            kv = turn_columns(now, key_value, cores, chips)
            kv_core = [
                lax.ppermute(kv[k], "branch", branch_target(experts, cores, k, 0))
                for k in range(1, cores)
            ]
            gate_in, kv = lax.optimization_barrier((gate_in, kv))
        if t == min(2, last):
            gate_in, kv_core = lax.optimization_barrier((gate_in, kv_core))
            kv_sum = kv[0].astype(F32) + sum(x.astype(F32) for x in kv_core)
            kv_chip = [
                lax.ppermute(
                    kv_sum[k].astype(BF16), "branch", branch_target(experts, cores, 0, k)
                )
                for k in range(1, chips)
            ]
        if t == min(5, last):
            gate_in, kv_chip = lax.optimization_barrier((gate_in, kv_chip))
            kv_sum = kv_sum[0] + sum(x.astype(F32) for x in kv_chip)
            merged_kv = (kv_sum / experts).astype(BF16)
            gate_in, merged_kv = lax.optimization_barrier((gate_in, merged_kv))
        if t < last:
            gate_sum = (gate_in.astype(F32) + gates[t].astype(F32)).astype(BF16)
            up_sum = (up_in.astype(F32) + ups[t].astype(F32)).astype(BF16)

    hidden = hidden_rows(
        where, gate_in, up_in, gates[last], ups[last], tails, origin, sizes, parts
    )
    sent = []
    if cores > 1:
        others = down_product(hidden[:parts], weights).astype(BF16)
        others = others.reshape(cores - 1, -1, width)
        sent = [
            lax.ppermute(others[k - 1], "branch", branch_target(experts, cores, k, 0))
            for k in range(1, cores)
        ]
    mixed = down_product(hidden[-parts:], weights)
    mixed, sent = lax.optimization_barrier((mixed, sent))
    mixed = mixed + sum(x.astype(F32) for x in sent)

    mixed = mixed.astype(BF16).reshape(chips * shards, token_count, width)
    groups = [
        [(chip * cores + core) * shards + s for chip in range(chips) for s in range(shards)]
        for core in range(cores)
    ]
    mixed = lax.all_to_all(
        mixed, ("branch", "shard"), split_axis=0, concat_axis=0, axis_index_groups=groups, tiled=True
    )
    return jnp.sum(mixed.astype(F32), axis=0).astype(BF16), merged_kv


def solution(mesh):
    grid = mesh.devices
    order = ring_order(list(grid[0, :]))
    cores = core_count(list(grid[:, 0]))
    return jax.shard_map(
        functools.partial(local, order, cores),
        mesh=mesh,
        in_specs=(
            P(("branch", "shard"), None),
            P(("branch", "shard"), None),
            P(("branch", "shard"), None),
            P("branch", "shard", None),
            P("branch", "shard", None),
            P("branch", "shard", None),
            P("branch", "shard", None),
        ),
        out_specs=(P(("branch", "shard"), None), P("shard", "branch")),
        check_vma=False,
    )
```

```python
import functools

import jax
import jax.numpy as jnp
import numpy as np
from jax import lax
from jax.experimental import pallas as pl
from jax.experimental.pallas import tpu as pltpu
from jax.sharding import PartitionSpec as P

F32 = jnp.float32
BF16 = jnp.bfloat16
LANES = 128
VMEM_LIMIT = 40 * 1024 * 1024
HIDDEN_LIMIT = 24 * 1024 * 1024


def ring_order(devices):
    places = [getattr(d, "coords", None) for d in devices]
    count = len(places)
    if any(p is None for p in places):
        return list(range(count))
    at = {(p[2], p[0]): i for i, p in enumerate(places)}
    zs, xs = sorted({k[0] for k in at}), sorted({k[1] for k in at})
    if len(at) != count or len(zs) * len(xs) != count or len(xs) < 2 or len(zs) % 2:
        return list(range(count))
    order = [at[(z, xs[0])] for z in zs]
    for i, z in enumerate(reversed(zs)):
        line = xs[1:] if i % 2 == 0 else list(reversed(xs[1:]))
        order += [at[(z, x)] for x in line]
    return order


def core_count(devices):
    places = [getattr(d, "coords", None) for d in devices]
    if any(p is None for p in places):
        return 1
    same = [tuple(p) == tuple(places[0]) for p in places]
    cores = sum(same)
    return cores if all(same[:cores]) and len(places) % cores == 0 else 1


def turned(index, step, count):
    return lax.rem(index + step, jnp.int32(count))


def place_rows(tokens, routes, mixing, experts, capacity, shards):
    token_count, width = tokens.shape
    depth = width // shards
    padded = -(-capacity // 8) * 8

    def kernel(tokens_ref, routes_ref, mixing_ref, out_ref):
        ids = [routes_ref[p % 2, p // 2] for p in range(2 * token_count)]
        slots = []
        for p in range(2 * token_count):
            slot = jnp.int32(0)
            for q in range(p):
                slot = slot + jnp.where(ids[q] == ids[p], 1, 0)
            slots.append(slot)
        row = lax.broadcasted_iota(jnp.int32, (padded, LANES), 0)
        lane = lax.broadcasted_iota(jnp.int32, (padded, LANES), 1)
        wide_row = lax.broadcasted_iota(jnp.int32, (padded, width), 0)
        values = tokens_ref[...].astype(F32)
        tails = []
        for p in range(2 * token_count):
            weight = jnp.full((padded, LANES), mixing_ref[p % 2, p // 2], F32)
            high = weight.astype(BF16).astype(F32)
            number = jnp.full((padded, LANES), float(p // 2 + 1), F32)
            tail = jnp.where(lane == 1, high, jnp.where(lane == 2, weight - high, 0.0))
            tails.append(jnp.where(lane == 0, number, tail))
        for e in range(experts):
            tail = jnp.zeros((padded, LANES), F32)
            body = jnp.zeros((padded, width), F32)
            for p in range(2 * token_count):
                slot = jnp.where(ids[p] == e, slots[p], -1)
                value = jnp.broadcast_to(values[p // 2 : p // 2 + 1], (padded, width))
                tail = jnp.where(row == slot, tails[p], tail)
                body = jnp.where(wide_row == slot, value, body)
            body, tail = body.astype(BF16)[:capacity], tail.astype(BF16)[:capacity]
            for s in range(shards):
                out_ref[e * shards + s, :, :depth] = body[:, s * depth : (s + 1) * depth]
                out_ref[e * shards + s, :, depth:] = tail

    return pl.pallas_call(
        kernel,
        out_shape=jax.ShapeDtypeStruct((experts * shards, capacity, depth + LANES), BF16),
        in_specs=[
            pl.BlockSpec(memory_space=pltpu.VMEM),
            pl.BlockSpec(memory_space=pltpu.SMEM),
            pl.BlockSpec(memory_space=pltpu.SMEM),
        ],
        out_specs=pl.BlockSpec(memory_space=pltpu.VMEM),
        name="place_rows",
    )(tokens, routes.T, mixing.T)


def column_pieces(where, table, rows, gate_weight, up_weight, first, pieces, cuts):
    count, depth = rows.shape
    cores, shards = table.shape[0], table.shape[2]
    width = gate_weight.shape[2] // shards
    block = width // cuts

    def kernel(where_ref, rows_ref, *refs):
        weights, outs = refs[: 2 * pieces], refs[2 * pieces :]
        for ref, out in zip(weights, outs):
            value = jnp.dot(rows_ref[...], ref[0], preferred_element_type=F32)
            out[...] = value.astype(BF16)

    def weight_map(side, i):
        def index(j, where_ref):
            key = lax.rem(where_ref[0], jnp.int32(cores)) * shards + where_ref[1]
            piece = jnp.int32(0)
            for n, value in enumerate(table[:, side, :, first + i].reshape(-1).tolist()):
                piece = jnp.where(key == n, jnp.int32(value), piece)
            return 0, 0, piece * cuts + j

        return pl.BlockSpec((1, depth, block), index)

    both = [(side, i) for side in range(2) for i in range(pieces)]
    out = pl.pallas_call(
        kernel,
        out_shape=[jax.ShapeDtypeStruct((count, width), BF16)] * len(both),
        grid_spec=pltpu.PrefetchScalarGridSpec(
            num_scalar_prefetch=1,
            grid=(cuts,),
            in_specs=[pl.BlockSpec((count, depth), lambda j, *_: (0, 0))]
            + [weight_map(side, i) for side, i in both],
            out_specs=[pl.BlockSpec((count, block), lambda j, *_: (0, j))] * len(both),
        ),
        compiler_params=pltpu.CompilerParams(vmem_limit_bytes=VMEM_LIMIT),
        cost_estimate=pl.CostEstimate(
            flops=4 * pieces * count * depth * width,
            bytes_accessed=4 * pieces * depth * width,
            transcendentals=0,
        ),
        name="column_pieces",
    )(where, rows, *([gate_weight] * pieces + [up_weight] * pieces))
    return out[:pieces], out[pieces:]


def plain_pieces(where, table, rows, gate_weight, up_weight):
    cores, shards = table.shape[0], table.shape[2]
    width = gate_weight.shape[2] // shards
    both = []
    for side, weight in enumerate((gate_weight, up_weight)):
        value = jnp.dot(rows, weight[0], preferred_element_type=F32).astype(BF16)
        at = jnp.asarray(table)[where[0] % cores, side, where[1]] * width
        both.append([lax.dynamic_slice_in_dim(value, at[t], width, 1) for t in range(shards)])
    return both


def turn_columns(where, x, cores, chips):
    rows, total = x.shape[1:]
    block = total // (cores * chips)

    def index(k):
        def place(i, where_ref):
            b = where_ref[0]
            chip = turned(lax.div(b, jnp.int32(cores)), i, chips)
            return 0, 0, chip * cores + turned(lax.rem(b, jnp.int32(cores)), k, cores)

        return place

    def kernel(where_ref, *refs):
        for k in range(cores):
            refs[cores + k][...] = refs[k][...]

    return pl.pallas_call(
        kernel,
        out_shape=[jax.ShapeDtypeStruct((chips, rows, block), x.dtype)] * cores,
        grid_spec=pltpu.PrefetchScalarGridSpec(
            num_scalar_prefetch=1,
            grid=(chips,),
            in_specs=[pl.BlockSpec((1, rows, block), index(k)) for k in range(cores)],
            out_specs=[pl.BlockSpec((1, rows, block), lambda i, *_: (i, 0, 0))] * cores,
        ),
        cost_estimate=pl.CostEstimate(flops=0, bytes_accessed=4 * rows * total, transcendentals=0),
        name="turn_columns",
    )(where, *([x] * cores))


def hidden_rows(where, gate_in, up_in, gate_own, up_own, tails, origin, sizes, parts):
    experts, shards, cores, token_count = sizes
    chips = experts // cores
    total = experts * shards * token_count
    kept = total // cores
    count, slice_width = gate_own.shape
    cut_width = slice_width // parts
    chunk = next(c for c in (256, LANES, cut_width) if cut_width % c == 0)

    def kernel(where_ref, gate_ref, up_ref, gate_own_ref, up_own_ref, tail_ref, origin_ref, *outs):
        tail = tail_ref[...].astype(F32)
        number, weight = tail[:, 0:1], tail[:, 1:2] + tail[:, 2:3]
        place = origin_ref[...]
        core = place[:, 0:1] - lax.rem(where_ref[0], jnp.int32(cores)).astype(F32)
        core = jnp.where(core < 0, core + cores, core)
        target = (core * chips + place[:, 1:2]) * shards + place[:, 2:3]
        target = target * token_count + number - 1.0
        target = jnp.where(number > 0, target, -1.0).astype(jnp.int32)
        spread = target == lax.broadcasted_iota(jnp.int32, (count, total), 1)
        spread = spread.astype(F32).astype(BF16)
        for at in range(0, slice_width, chunk):
            cut = slice(at, at + chunk)
            gate = gate_ref[:, cut].astype(F32) + gate_own_ref[:, cut].astype(F32)
            upper = up_ref[:, cut].astype(F32) + up_own_ref[:, cut].astype(F32)
            hidden = (gate / (1.0 + jnp.exp(-gate)) * upper * weight).astype(BF16)
            hidden = lax.dot_general(
                spread, hidden, (((0,), (0,)), ((), ())), preferred_element_type=F32
            ).astype(BF16)
            part, to = at // cut_width, at % cut_width
            if cores > 1:
                outs[part][:, to : to + chunk] = hidden[kept:]
            outs[len(outs) - parts + part][:, to : to + chunk] = hidden[:kept]

    shapes = [jax.ShapeDtypeStruct((kept, cut_width), BF16)] * parts
    if cores > 1:
        shapes = [jax.ShapeDtypeStruct((total - kept, cut_width), BF16)] * parts + shapes
    return pl.pallas_call(
        kernel,
        out_shape=shapes,
        in_specs=[pl.BlockSpec(memory_space=pltpu.SMEM)]
        + [pl.BlockSpec(memory_space=pltpu.VMEM)] * 6,
        out_specs=[pl.BlockSpec(memory_space=pltpu.VMEM)] * len(shapes),
        cost_estimate=pl.CostEstimate(
            flops=2 * total * slice_width * count,
            bytes_accessed=8 * count * slice_width,
            transcendentals=count * slice_width,
        ),
        compiler_params=pltpu.CompilerParams(vmem_limit_bytes=HIDDEN_LIMIT),
        name="hidden_rows",
    )(where, gate_in, up_in, gate_own, up_own, tails, origin)


def down_product(hidden, weights):
    return sum(jnp.dot(h, w, preferred_element_type=F32) for h, w in zip(hidden, weights))


def branch_target(size, cores, core_step, chip_step):
    chips = size // cores
    return [
        (i, (i // cores + chip_step) % chips * cores + (i + core_step) % cores)
        for i in range(size)
    ]


def local(order, cores, tokens, routes, mixing, gate_weight, up_weight, down_weight, key_value):
    experts = lax.axis_size("branch")
    shards = lax.axis_size("shard")
    chips = experts // cores
    token_count, width = tokens.shape
    capacity = max(2, (2 * token_count + experts - 1) // experts + 1)
    depth = gate_weight.shape[1]
    slice_width = down_weight.shape[1]
    count = experts * shards * capacity
    sizes = (experts, shards, cores, token_count)
    where = jnp.stack([lax.axis_index("branch"), lax.axis_index("shard")]).astype(jnp.int32)

    place = np.argsort(np.asarray(order))
    table = np.zeros((cores, 2, shards, shards), np.int32)
    pairs = [[], []]
    for side in range(2):
        for b in range(experts):
            core = b % cores
            way = 1 if (side + core) % 2 == 0 else -1
            for s in range(shards):
                for t in range(shards):
                    table[core, side, s, t] = order[(place[s] - way * (1 + t)) % shards]
                pairs[side].append((b * shards + s, b * shards + order[(place[s] + way) % shards]))
    source = np.arange(count) // capacity
    origin = np.zeros((count, LANES), np.float32)
    origin[:, 0] = source // shards % cores
    origin[:, 1] = source // shards // cores
    origin[:, 2] = source % shards
    origin = jnp.asarray(origin)

    cells = place_rows(tokens, routes, mixing, experts, capacity, shards)
    cells, where, origin = lax.optimization_barrier((cells, where, origin))
    cells = lax.all_to_all(cells, ("branch", "shard"), split_axis=0, concat_axis=0, tiled=True)
    cells = cells.reshape(count, depth + LANES)
    rows, tails = cells[:, :depth], cells[:, depth:]

    sliced = slice_width % LANES == 0
    if sliced:
        cuts = 2 if slice_width % (2 * LANES) == 0 else 1
        gates, ups = column_pieces(where, table, rows, gate_weight, up_weight, 0, 1, cuts)
    else:
        gates, ups = plain_pieces(where, table, rows, gate_weight, up_weight)
    gate_sum, up_sum = gates[0], ups[0]
    last = shards - 1
    parts = 1
    weights = [down_weight[0]]
    for t in range(1, shards):
        now, gate_sum = lax.optimization_barrier((where, gate_sum))
        gate_in = lax.ppermute(gate_sum, ("branch", "shard"), pairs[0])
        up_in = lax.ppermute(up_sum, ("branch", "shard"), pairs[1])
        if sliced and len(gates) < shards:
            more = column_pieces(
                now, table, rows, gate_weight, up_weight, len(gates), 1, cuts
            )
            gates, ups = gates + more[0], ups + more[1]
        if t == 1:
            kv = turn_columns(now, key_value, cores, chips)
            kv_core = [
                lax.ppermute(kv[k], "branch", branch_target(experts, cores, k, 0))
                for k in range(1, cores)
            ]
            gate_in, kv = lax.optimization_barrier((gate_in, kv))
        if t == min(2, last):
            gate_in, kv_core = lax.optimization_barrier((gate_in, kv_core))
            kv_sum = kv[0].astype(F32) + sum(x.astype(F32) for x in kv_core)
            kv_chip = [
                lax.ppermute(
                    kv_sum[k].astype(BF16), "branch", branch_target(experts, cores, 0, k)
                )
                for k in range(1, chips)
            ]
        if t == min(5, last):
            gate_in, kv_chip = lax.optimization_barrier((gate_in, kv_chip))
            kv_sum = kv_sum[0] + sum(x.astype(F32) for x in kv_chip)
            merged_kv = (kv_sum / experts).astype(BF16)
            gate_in, merged_kv = lax.optimization_barrier((gate_in, merged_kv))
        if t < last:
            gate_sum = (gate_in.astype(F32) + gates[t].astype(F32)).astype(BF16)
            up_sum = (up_in.astype(F32) + ups[t].astype(F32)).astype(BF16)

    hidden = hidden_rows(
        where, gate_in, up_in, gates[last], ups[last], tails, origin, sizes, parts
    )
    sent = []
    if cores > 1:
        others = down_product(hidden[:parts], weights).astype(BF16)
        others = others.reshape(cores - 1, -1, width)
        sent = [
            lax.ppermute(others[k - 1], "branch", branch_target(experts, cores, k, 0))
            for k in range(1, cores)
        ]
    mixed = down_product(hidden[-parts:], weights)
    mixed, sent = lax.optimization_barrier((mixed, sent))
    mixed = mixed + sum(x.astype(F32) for x in sent)

    mixed = mixed.astype(BF16).reshape(chips * shards, token_count, width)
    groups = [
        [(chip * cores + core) * shards + s for chip in range(chips) for s in range(shards)]
        for core in range(cores)
    ]
    mixed = lax.all_to_all(
        mixed, ("branch", "shard"), split_axis=0, concat_axis=0, axis_index_groups=groups, tiled=True
    )
    return jnp.sum(mixed.astype(F32), axis=0).astype(BF16), merged_kv


def solution(mesh):
    grid = mesh.devices
    order = ring_order(list(grid[0, :]))
    cores = core_count(list(grid[:, 0]))
    return jax.shard_map(
        functools.partial(local, order, cores),
        mesh=mesh,
        in_specs=(
            P(("branch", "shard"), None),
            P(("branch", "shard"), None),
            P(("branch", "shard"), None),
            P("branch", "shard", None),
            P("branch", "shard", None),
            P("branch", "shard", None),
            P("branch", "shard", None),
        ),
        out_specs=(P(("branch", "shard"), None), P("shard", "branch")),
        check_vma=False,
    )
```

```python
import functools

import jax
import jax.numpy as jnp
import numpy as np
from jax import lax
from jax.experimental import pallas as pl
from jax.experimental.pallas import tpu as pltpu
from jax.sharding import PartitionSpec as P

F32 = jnp.float32
BF16 = jnp.bfloat16
LANES = 128
VMEM_LIMIT = 40 * 1024 * 1024
HIDDEN_LIMIT = 24 * 1024 * 1024


def ring_order(devices):
    places = [getattr(d, "coords", None) for d in devices]
    count = len(places)
    if any(p is None for p in places):
        return list(range(count))
    at = {(p[2], p[0]): i for i, p in enumerate(places)}
    zs, xs = sorted({k[0] for k in at}), sorted({k[1] for k in at})
    if len(at) != count or len(zs) * len(xs) != count or len(xs) < 2 or len(zs) % 2:
        return list(range(count))
    order = [at[(z, xs[0])] for z in zs]
    for i, z in enumerate(reversed(zs)):
        line = xs[1:] if i % 2 == 0 else list(reversed(xs[1:]))
        order += [at[(z, x)] for x in line]
    return order


def core_count(devices):
    places = [getattr(d, "coords", None) for d in devices]
    if any(p is None for p in places):
        return 1
    same = [tuple(p) == tuple(places[0]) for p in places]
    cores = sum(same)
    return cores if all(same[:cores]) and len(places) % cores == 0 else 1


def turned(index, step, count):
    return lax.rem(index + step, jnp.int32(count))


def place_rows(tokens, routes, mixing, experts, capacity, shards):
    token_count, width = tokens.shape
    depth = width // shards
    padded = -(-capacity // 8) * 8

    def kernel(tokens_ref, routes_ref, mixing_ref, out_ref):
        ids = [routes_ref[p % 2, p // 2] for p in range(2 * token_count)]
        slots = []
        for p in range(2 * token_count):
            slot = jnp.int32(0)
            for q in range(p):
                slot = slot + jnp.where(ids[q] == ids[p], 1, 0)
            slots.append(slot)
        row = lax.broadcasted_iota(jnp.int32, (padded, LANES), 0)
        lane = lax.broadcasted_iota(jnp.int32, (padded, LANES), 1)
        wide_row = lax.broadcasted_iota(jnp.int32, (padded, width), 0)
        values = tokens_ref[...].astype(F32)
        tails = []
        for p in range(2 * token_count):
            weight = jnp.full((padded, LANES), mixing_ref[p % 2, p // 2], F32)
            high = weight.astype(BF16).astype(F32)
            number = jnp.full((padded, LANES), float(p // 2 + 1), F32)
            tail = jnp.where(lane == 1, high, jnp.where(lane == 2, weight - high, 0.0))
            tails.append(jnp.where(lane == 0, number, tail))
        for e in range(experts):
            tail = jnp.zeros((padded, LANES), F32)
            body = jnp.zeros((padded, width), F32)
            for p in range(2 * token_count):
                slot = jnp.where(ids[p] == e, slots[p], -1)
                value = jnp.broadcast_to(values[p // 2 : p // 2 + 1], (padded, width))
                tail = jnp.where(row == slot, tails[p], tail)
                body = jnp.where(wide_row == slot, value, body)
            body, tail = body.astype(BF16)[:capacity], tail.astype(BF16)[:capacity]
            for s in range(shards):
                out_ref[e * shards + s, :, :depth] = body[:, s * depth : (s + 1) * depth]
                out_ref[e * shards + s, :, depth:] = tail

    return pl.pallas_call(
        kernel,
        out_shape=jax.ShapeDtypeStruct((experts * shards, capacity, depth + LANES), BF16),
        in_specs=[
            pl.BlockSpec(memory_space=pltpu.VMEM),
            pl.BlockSpec(memory_space=pltpu.SMEM),
            pl.BlockSpec(memory_space=pltpu.SMEM),
        ],
        out_specs=pl.BlockSpec(memory_space=pltpu.VMEM),
        name="place_rows",
    )(tokens, routes.T, mixing.T)


def column_pieces(where, table, rows, gate_weight, up_weight, first, pieces, cuts):
    count, depth = rows.shape
    shards = table.shape[1]
    width = gate_weight.shape[2] // shards
    block = width // cuts

    def kernel(where_ref, rows_ref, *refs):
        weights, outs = refs[: 2 * pieces], refs[2 * pieces :]
        for ref, out in zip(weights, outs):
            value = jnp.dot(rows_ref[...], ref[0], preferred_element_type=F32)
            out[...] = value.astype(BF16)

    def weight_map(side, i):
        def index(j, where_ref):
            piece = jnp.int32(0)
            for s, value in enumerate(table[side, :, first + i].tolist()):
                piece = jnp.where(where_ref[1] == s, jnp.int32(value), piece)
            return 0, 0, piece * cuts + j

        return pl.BlockSpec((1, depth, block), index)

    both = [(side, i) for side in range(2) for i in range(pieces)]
    out = pl.pallas_call(
        kernel,
        out_shape=[jax.ShapeDtypeStruct((count, width), BF16)] * len(both),
        grid_spec=pltpu.PrefetchScalarGridSpec(
            num_scalar_prefetch=1,
            grid=(cuts,),
            in_specs=[pl.BlockSpec((count, depth), lambda j, *_: (0, 0))]
            + [weight_map(side, i) for side, i in both],
            out_specs=[pl.BlockSpec((count, block), lambda j, *_: (0, j))] * len(both),
        ),
        compiler_params=pltpu.CompilerParams(vmem_limit_bytes=VMEM_LIMIT),
        cost_estimate=pl.CostEstimate(
            flops=4 * pieces * count * depth * width,
            bytes_accessed=4 * pieces * depth * width,
            transcendentals=0,
        ),
        name="column_pieces",
    )(where, rows, *([gate_weight] * pieces + [up_weight] * pieces))
    return out[:pieces], out[pieces:]


def plain_pieces(where, table, rows, gate_weight, up_weight):
    shards = table.shape[1]
    width = gate_weight.shape[2] // shards
    both = []
    for side, weight in enumerate((gate_weight, up_weight)):
        value = jnp.dot(rows, weight[0], preferred_element_type=F32).astype(BF16)
        at = jnp.asarray(table)[side, where[1]] * width
        both.append([lax.dynamic_slice_in_dim(value, at[t], width, 1) for t in range(shards)])
    return both


def turn_columns(where, x, cores, chips):
    rows, total = x.shape[1:]
    block = total // (cores * chips)

    def index(k):
        def place(i, where_ref):
            b = where_ref[0]
            chip = turned(lax.div(b, jnp.int32(cores)), i, chips)
            return 0, 0, chip * cores + turned(lax.rem(b, jnp.int32(cores)), k, cores)

        return place

    def kernel(where_ref, *refs):
        for k in range(cores):
            refs[cores + k][...] = refs[k][...]

    return pl.pallas_call(
        kernel,
        out_shape=[jax.ShapeDtypeStruct((chips, rows, block), x.dtype)] * cores,
        grid_spec=pltpu.PrefetchScalarGridSpec(
            num_scalar_prefetch=1,
            grid=(chips,),
            in_specs=[pl.BlockSpec((1, rows, block), index(k)) for k in range(cores)],
            out_specs=[pl.BlockSpec((1, rows, block), lambda i, *_: (i, 0, 0))] * cores,
        ),
        cost_estimate=pl.CostEstimate(flops=0, bytes_accessed=4 * rows * total, transcendentals=0),
        name="turn_columns",
    )(where, *([x] * cores))


def hidden_rows(where, gate_in, up_in, gate_own, up_own, tails, origin, sizes, parts):
    experts, shards, cores, token_count = sizes
    chips = experts // cores
    total = experts * shards * token_count
    kept = total // cores
    count, slice_width = gate_own.shape
    cut_width = slice_width // parts
    chunk = next(c for c in (256, LANES, cut_width) if cut_width % c == 0)

    def kernel(where_ref, gate_ref, up_ref, gate_own_ref, up_own_ref, tail_ref, origin_ref, *outs):
        tail = tail_ref[...].astype(F32)
        number, weight = tail[:, 0:1], tail[:, 1:2] + tail[:, 2:3]
        place = origin_ref[...]
        core = place[:, 0:1] - lax.rem(where_ref[0], jnp.int32(cores)).astype(F32)
        core = jnp.where(core < 0, core + cores, core)
        target = (core * chips + place[:, 1:2]) * shards + place[:, 2:3]
        target = target * token_count + number - 1.0
        target = jnp.where(number > 0, target, -1.0).astype(jnp.int32)
        spread = target == lax.broadcasted_iota(jnp.int32, (count, total), 1)
        spread = spread.astype(F32).astype(BF16)
        for at in range(0, slice_width, chunk):
            cut = slice(at, at + chunk)
            gate = gate_ref[:, cut].astype(F32) + gate_own_ref[:, cut].astype(F32)
            upper = up_ref[:, cut].astype(F32) + up_own_ref[:, cut].astype(F32)
            hidden = (gate / (1.0 + jnp.exp(-gate)) * upper * weight).astype(BF16)
            hidden = lax.dot_general(
                spread, hidden, (((0,), (0,)), ((), ())), preferred_element_type=F32
            ).astype(BF16)
            part, to = at // cut_width, at % cut_width
            if cores > 1:
                outs[part][:, to : to + chunk] = hidden[kept:]
            outs[len(outs) - parts + part][:, to : to + chunk] = hidden[:kept]

    shapes = [jax.ShapeDtypeStruct((kept, cut_width), BF16)] * parts
    if cores > 1:
        shapes = [jax.ShapeDtypeStruct((total - kept, cut_width), BF16)] * parts + shapes
    return pl.pallas_call(
        kernel,
        out_shape=shapes,
        in_specs=[pl.BlockSpec(memory_space=pltpu.SMEM)]
        + [pl.BlockSpec(memory_space=pltpu.VMEM)] * 6,
        out_specs=[pl.BlockSpec(memory_space=pltpu.VMEM)] * len(shapes),
        cost_estimate=pl.CostEstimate(
            flops=2 * total * slice_width * count,
            bytes_accessed=8 * count * slice_width,
            transcendentals=count * slice_width,
        ),
        compiler_params=pltpu.CompilerParams(vmem_limit_bytes=HIDDEN_LIMIT),
        name="hidden_rows",
    )(where, gate_in, up_in, gate_own, up_own, tails, origin)


def down_product(hidden, weights):
    return sum(jnp.dot(h, w, preferred_element_type=F32) for h, w in zip(hidden, weights))


def branch_target(size, cores, core_step, chip_step):
    chips = size // cores
    return [
        (i, (i // cores + chip_step) % chips * cores + (i + core_step) % cores)
        for i in range(size)
    ]


def local(order, cores, tokens, routes, mixing, gate_weight, up_weight, down_weight, key_value):
    experts = lax.axis_size("branch")
    shards = lax.axis_size("shard")
    chips = experts // cores
    token_count, width = tokens.shape
    capacity = max(2, (2 * token_count + experts - 1) // experts + 1)
    depth = gate_weight.shape[1]
    slice_width = down_weight.shape[1]
    count = experts * shards * capacity
    sizes = (experts, shards, cores, token_count)
    where = jnp.stack([lax.axis_index("branch"), lax.axis_index("shard")]).astype(jnp.int32)

    place = np.argsort(np.asarray(order))
    table = np.zeros((2, shards, shards), np.int32)
    pairs = []
    for side, way in enumerate((1, -1)):
        for s in range(shards):
            for t in range(shards):
                table[side, s, t] = order[(place[s] - way * (1 + t)) % shards]
        pairs.append([(s, order[(place[s] + way) % shards]) for s in range(shards)])
    source = np.arange(count) // capacity
    origin = np.zeros((count, LANES), np.float32)
    origin[:, 0] = source // shards % cores
    origin[:, 1] = source // shards // cores
    origin[:, 2] = source % shards
    origin = jnp.asarray(origin)

    cells = place_rows(tokens, routes, mixing, experts, capacity, shards)
    cells, where, origin = lax.optimization_barrier((cells, where, origin))
    cells = lax.all_to_all(cells, ("branch", "shard"), split_axis=0, concat_axis=0, tiled=True)
    cells = cells.reshape(count, depth + LANES)
    rows, tails = cells[:, :depth], cells[:, depth:]

    sliced = slice_width % LANES == 0
    if sliced:
        cuts = 2 if slice_width % (2 * LANES) == 0 else 1
        gates, ups = column_pieces(where, table, rows, gate_weight, up_weight, 0, 1, cuts)
    else:
        gates, ups = plain_pieces(where, table, rows, gate_weight, up_weight)
    gate_sum, up_sum = gates[0], ups[0]
    last = shards - 1
    parts = 1
    weights = [down_weight[0]]
    for t in range(1, shards):
        now, gate_sum = lax.optimization_barrier((where, gate_sum))
        gate_in = lax.ppermute(gate_sum, "shard", pairs[0])
        up_in = lax.ppermute(up_sum, "shard", pairs[1])
        if sliced and len(gates) < shards:
            more = column_pieces(
                now, table, rows, gate_weight, up_weight, len(gates), 1, cuts
            )
            gates, ups = gates + more[0], ups + more[1]
        if t == min(2, last):
            kv = turn_columns(now, key_value, cores, chips)
            kv_core = [
                lax.ppermute(kv[k], "branch", branch_target(experts, cores, k, 0))
                for k in range(1, cores)
            ]
            gate_in, kv = lax.optimization_barrier((gate_in, kv))
        if t == min(3, last):
            gate_in, kv_core = lax.optimization_barrier((gate_in, kv_core))
            kv_sum = kv[0].astype(F32) + sum(x.astype(F32) for x in kv_core)
            kv_chip = [
                lax.ppermute(
                    kv_sum[k].astype(BF16), "branch", branch_target(experts, cores, 0, k)
                )
                for k in range(1, chips)
            ]
        if t == min(6, last):
            gate_in, kv_chip = lax.optimization_barrier((gate_in, kv_chip))
            kv_sum = kv_sum[0] + sum(x.astype(F32) for x in kv_chip)
            merged_kv = (kv_sum / experts).astype(BF16)
            gate_in, merged_kv = lax.optimization_barrier((gate_in, merged_kv))
        if t < last:
            gate_sum = (gate_in.astype(F32) + gates[t].astype(F32)).astype(BF16)
            up_sum = (up_in.astype(F32) + ups[t].astype(F32)).astype(BF16)

    hidden = hidden_rows(
        where, gate_in, up_in, gates[last], ups[last], tails, origin, sizes, parts
    )
    sent = []
    if cores > 1:
        others = down_product(hidden[:parts], weights).astype(BF16)
        others = others.reshape(cores - 1, -1, width)
        sent = [
            lax.ppermute(others[k - 1], "branch", branch_target(experts, cores, k, 0))
            for k in range(1, cores)
        ]
    mixed = down_product(hidden[-parts:], weights)
    mixed, sent = lax.optimization_barrier((mixed, sent))
    mixed = mixed + sum(x.astype(F32) for x in sent)

    mixed = mixed.astype(BF16).reshape(chips * shards, token_count, width)
    groups = [
        [(chip * cores + core) * shards + s for chip in range(chips) for s in range(shards)]
        for core in range(cores)
    ]
    mixed = lax.all_to_all(
        mixed, ("branch", "shard"), split_axis=0, concat_axis=0, axis_index_groups=groups, tiled=True
    )
    return jnp.sum(mixed.astype(F32), axis=0).astype(BF16), merged_kv


def solution(mesh):
    grid = mesh.devices
    order = ring_order(list(grid[0, :]))
    cores = core_count(list(grid[:, 0]))
    return jax.shard_map(
        functools.partial(local, order, cores),
        mesh=mesh,
        in_specs=(
            P(("branch", "shard"), None),
            P(("branch", "shard"), None),
            P(("branch", "shard"), None),
            P("branch", "shard", None),
            P("branch", "shard", None),
            P("branch", "shard", None),
            P("branch", "shard", None),
        ),
        out_specs=(P(("branch", "shard"), None), P("shard", "branch")),
        check_vma=False,
    )
```

```python
import functools

import jax
import jax.numpy as jnp
import numpy as np
from jax import lax
from jax.experimental import pallas as pl
from jax.experimental.pallas import tpu as pltpu
from jax.sharding import PartitionSpec as P

F32 = jnp.float32
BF16 = jnp.bfloat16
LANES = 128
VMEM_LIMIT = 40 * 1024 * 1024
HIDDEN_LIMIT = 24 * 1024 * 1024


def ring_order(devices):
    places = [getattr(d, "coords", None) for d in devices]
    count = len(places)
    if any(p is None for p in places):
        return list(range(count))
    at = {(p[2], p[0]): i for i, p in enumerate(places)}
    zs, xs = sorted({k[0] for k in at}), sorted({k[1] for k in at})
    if len(at) != count or len(zs) * len(xs) != count or len(xs) < 2 or len(zs) % 2:
        return list(range(count))
    order = [at[(z, xs[0])] for z in zs]
    for i, z in enumerate(reversed(zs)):
        line = xs[1:] if i % 2 == 0 else list(reversed(xs[1:]))
        order += [at[(z, x)] for x in line]
    return order


def core_count(devices):
    places = [getattr(d, "coords", None) for d in devices]
    if any(p is None for p in places):
        return 1
    same = [tuple(p) == tuple(places[0]) for p in places]
    cores = sum(same)
    return cores if all(same[:cores]) and len(places) % cores == 0 else 1


def turned(index, step, count):
    return lax.rem(index + step, jnp.int32(count))


def place_rows(tokens, routes, mixing, experts, capacity, shards):
    token_count, width = tokens.shape
    depth = width // shards
    padded = -(-capacity // 8) * 8

    def kernel(tokens_ref, routes_ref, mixing_ref, out_ref):
        ids = [routes_ref[p % 2, p // 2] for p in range(2 * token_count)]
        slots = []
        for p in range(2 * token_count):
            slot = jnp.int32(0)
            for q in range(p):
                slot = slot + jnp.where(ids[q] == ids[p], 1, 0)
            slots.append(slot)
        row = lax.broadcasted_iota(jnp.int32, (padded, LANES), 0)
        lane = lax.broadcasted_iota(jnp.int32, (padded, LANES), 1)
        wide_row = lax.broadcasted_iota(jnp.int32, (padded, width), 0)
        values = tokens_ref[...].astype(F32)
        tails = []
        for p in range(2 * token_count):
            weight = jnp.full((padded, LANES), mixing_ref[p % 2, p // 2], F32)
            high = weight.astype(BF16).astype(F32)
            number = jnp.full((padded, LANES), float(p // 2 + 1), F32)
            tail = jnp.where(lane == 1, high, jnp.where(lane == 2, weight - high, 0.0))
            tails.append(jnp.where(lane == 0, number, tail))
        for e in range(experts):
            tail = jnp.zeros((padded, LANES), F32)
            body = jnp.zeros((padded, width), F32)
            for p in range(2 * token_count):
                slot = jnp.where(ids[p] == e, slots[p], -1)
                value = jnp.broadcast_to(values[p // 2 : p // 2 + 1], (padded, width))
                tail = jnp.where(row == slot, tails[p], tail)
                body = jnp.where(wide_row == slot, value, body)
            body, tail = body.astype(BF16)[:capacity], tail.astype(BF16)[:capacity]
            for s in range(shards):
                out_ref[e * shards + s, :, :depth] = body[:, s * depth : (s + 1) * depth]
                out_ref[e * shards + s, :, depth:] = tail

    return pl.pallas_call(
        kernel,
        out_shape=jax.ShapeDtypeStruct((experts * shards, capacity, depth + LANES), BF16),
        in_specs=[
            pl.BlockSpec(memory_space=pltpu.VMEM),
            pl.BlockSpec(memory_space=pltpu.SMEM),
            pl.BlockSpec(memory_space=pltpu.SMEM),
        ],
        out_specs=pl.BlockSpec(memory_space=pltpu.VMEM),
        name="place_rows",
    )(tokens, routes.T, mixing.T)


def column_pieces(where, table, rows, gate_weight, up_weight, first, pieces, cuts):
    count, depth = rows.shape
    shards = table.shape[1]
    width = gate_weight.shape[2] // shards
    block = width // cuts

    def kernel(where_ref, rows_ref, *refs):
        weights, outs = refs[: 2 * pieces], refs[2 * pieces :]
        for ref, out in zip(weights, outs):
            value = jnp.dot(rows_ref[...], ref[0], preferred_element_type=F32)
            out[...] = value.astype(BF16)

    def weight_map(side, i):
        def index(j, where_ref):
            piece = jnp.int32(0)
            for s, value in enumerate(table[side, :, first + i].tolist()):
                piece = jnp.where(where_ref[1] == s, jnp.int32(value), piece)
            return 0, 0, piece * cuts + j

        return pl.BlockSpec((1, depth, block), index)

    both = [(side, i) for side in range(2) for i in range(pieces)]
    out = pl.pallas_call(
        kernel,
        out_shape=[jax.ShapeDtypeStruct((count, width), BF16)] * len(both),
        grid_spec=pltpu.PrefetchScalarGridSpec(
            num_scalar_prefetch=1,
            grid=(cuts,),
            in_specs=[pl.BlockSpec((count, depth), lambda j, *_: (0, 0))]
            + [weight_map(side, i) for side, i in both],
            out_specs=[pl.BlockSpec((count, block), lambda j, *_: (0, j))] * len(both),
        ),
        compiler_params=pltpu.CompilerParams(vmem_limit_bytes=VMEM_LIMIT),
        cost_estimate=pl.CostEstimate(
            flops=4 * pieces * count * depth * width,
            bytes_accessed=4 * pieces * depth * width,
            transcendentals=0,
        ),
        name="column_pieces",
    )(where, rows, *([gate_weight] * pieces + [up_weight] * pieces))
    return out[:pieces], out[pieces:]


def plain_pieces(where, table, rows, gate_weight, up_weight):
    shards = table.shape[1]
    width = gate_weight.shape[2] // shards
    both = []
    for side, weight in enumerate((gate_weight, up_weight)):
        value = jnp.dot(rows, weight[0], preferred_element_type=F32).astype(BF16)
        at = jnp.asarray(table)[side, where[1]] * width
        both.append([lax.dynamic_slice_in_dim(value, at[t], width, 1) for t in range(shards)])
    return both


def turn_columns(where, x, cores, chips):
    rows, total = x.shape[1:]
    block = total // (cores * chips)

    def index(k):
        def place(i, where_ref):
            b = where_ref[0]
            chip = turned(lax.div(b, jnp.int32(cores)), i, chips)
            return 0, 0, chip * cores + turned(lax.rem(b, jnp.int32(cores)), k, cores)

        return place

    def kernel(where_ref, *refs):
        for k in range(cores):
            refs[cores + k][...] = refs[k][...]

    return pl.pallas_call(
        kernel,
        out_shape=[jax.ShapeDtypeStruct((chips, rows, block), x.dtype)] * cores,
        grid_spec=pltpu.PrefetchScalarGridSpec(
            num_scalar_prefetch=1,
            grid=(chips,),
            in_specs=[pl.BlockSpec((1, rows, block), index(k)) for k in range(cores)],
            out_specs=[pl.BlockSpec((1, rows, block), lambda i, *_: (i, 0, 0))] * cores,
        ),
        cost_estimate=pl.CostEstimate(flops=0, bytes_accessed=4 * rows * total, transcendentals=0),
        name="turn_columns",
    )(where, *([x] * cores))


def hidden_rows(where, gate_in, up_in, gate_own, up_own, tails, origin, sizes, parts):
    experts, shards, cores, token_count = sizes
    chips = experts // cores
    total = experts * shards * token_count
    kept = total // cores
    count, slice_width = gate_own.shape
    cut_width = slice_width // parts
    chunk = next(c for c in (256, LANES, cut_width) if cut_width % c == 0)

    def kernel(where_ref, gate_ref, up_ref, gate_own_ref, up_own_ref, tail_ref, origin_ref, *outs):
        tail = tail_ref[...].astype(F32)
        number, weight = tail[:, 0:1], tail[:, 1:2] + tail[:, 2:3]
        place = origin_ref[...]
        core = place[:, 0:1] - lax.rem(where_ref[0], jnp.int32(cores)).astype(F32)
        core = jnp.where(core < 0, core + cores, core)
        target = (core * chips + place[:, 1:2]) * shards + place[:, 2:3]
        target = target * token_count + number - 1.0
        target = jnp.where(number > 0, target, -1.0).astype(jnp.int32)
        spread = target == lax.broadcasted_iota(jnp.int32, (count, total), 1)
        spread = spread.astype(F32).astype(BF16)
        for at in range(0, slice_width, chunk):
            cut = slice(at, at + chunk)
            gate = gate_ref[:, cut].astype(F32) + gate_own_ref[:, cut].astype(F32)
            upper = up_ref[:, cut].astype(F32) + up_own_ref[:, cut].astype(F32)
            hidden = (gate / (1.0 + jnp.exp(-gate)) * upper * weight).astype(BF16)
            hidden = lax.dot_general(
                spread, hidden, (((0,), (0,)), ((), ())), preferred_element_type=F32
            ).astype(BF16)
            part, to = at // cut_width, at % cut_width
            if cores > 1:
                outs[part][:, to : to + chunk] = hidden[kept:]
            outs[len(outs) - parts + part][:, to : to + chunk] = hidden[:kept]

    shapes = [jax.ShapeDtypeStruct((kept, cut_width), BF16)] * parts
    if cores > 1:
        shapes = [jax.ShapeDtypeStruct((total - kept, cut_width), BF16)] * parts + shapes
    return pl.pallas_call(
        kernel,
        out_shape=shapes,
        in_specs=[pl.BlockSpec(memory_space=pltpu.SMEM)]
        + [pl.BlockSpec(memory_space=pltpu.VMEM)] * 6,
        out_specs=[pl.BlockSpec(memory_space=pltpu.VMEM)] * len(shapes),
        cost_estimate=pl.CostEstimate(
            flops=2 * total * slice_width * count,
            bytes_accessed=8 * count * slice_width,
            transcendentals=count * slice_width,
        ),
        compiler_params=pltpu.CompilerParams(vmem_limit_bytes=HIDDEN_LIMIT),
        name="hidden_rows",
    )(where, gate_in, up_in, gate_own, up_own, tails, origin)


def down_product(hidden, weights):
    return sum(jnp.dot(h, w, preferred_element_type=F32) for h, w in zip(hidden, weights))


def branch_target(size, cores, core_step, chip_step):
    chips = size // cores
    return [
        (i, (i // cores + chip_step) % chips * cores + (i + core_step) % cores)
        for i in range(size)
    ]


def local(order, cores, tokens, routes, mixing, gate_weight, up_weight, down_weight, key_value):
    experts = lax.axis_size("branch")
    shards = lax.axis_size("shard")
    chips = experts // cores
    token_count, width = tokens.shape
    capacity = max(2, (2 * token_count + experts - 1) // experts + 1)
    depth = gate_weight.shape[1]
    slice_width = down_weight.shape[1]
    count = experts * shards * capacity
    sizes = (experts, shards, cores, token_count)
    where = jnp.stack([lax.axis_index("branch"), lax.axis_index("shard")]).astype(jnp.int32)

    place = np.argsort(np.asarray(order))
    table = np.zeros((2, shards, shards), np.int32)
    pairs = []
    for side, way in enumerate((1, -1)):
        for s in range(shards):
            for t in range(shards):
                table[side, s, t] = order[(place[s] - way * (1 + t)) % shards]
        pairs.append([(s, order[(place[s] + way) % shards]) for s in range(shards)])
    source = np.arange(count) // capacity
    origin = np.zeros((count, LANES), np.float32)
    origin[:, 0] = source // shards % cores
    origin[:, 1] = source // shards // cores
    origin[:, 2] = source % shards
    origin = jnp.asarray(origin)

    cells = place_rows(tokens, routes, mixing, experts, capacity, shards)
    cells, where, origin = lax.optimization_barrier((cells, where, origin))
    cells = lax.all_to_all(cells, ("branch", "shard"), split_axis=0, concat_axis=0, tiled=True)
    cells = cells.reshape(count, depth + LANES)
    rows, tails = cells[:, :depth], cells[:, depth:]

    sliced = slice_width % LANES == 0
    if sliced:
        cuts = 2 if slice_width % (2 * LANES) == 0 else 1
        gates, ups = column_pieces(where, table, rows, gate_weight, up_weight, 0, 1, cuts)
    else:
        gates, ups = plain_pieces(where, table, rows, gate_weight, up_weight)
    gate_sum, up_sum = gates[0], ups[0]
    last = shards - 1
    parts = 1
    weights = [down_weight[0]]
    for t in range(1, shards):
        now, gate_sum = lax.optimization_barrier((where, gate_sum))
        gate_in = lax.ppermute(gate_sum, "shard", pairs[0])
        up_in = lax.ppermute(up_sum, "shard", pairs[1])
        if sliced and len(gates) < shards:
            more = column_pieces(
                now, table, rows, gate_weight, up_weight, len(gates), 1, cuts
            )
            gates, ups = gates + more[0], ups + more[1]
        if t == 1:
            kv = turn_columns(now, key_value, cores, chips)
            kv_core = [
                lax.ppermute(kv[k], "branch", branch_target(experts, cores, k, 0))
                for k in range(1, cores)
            ]
            gate_in, kv = lax.optimization_barrier((gate_in, kv))
        if t == min(2, last):
            gate_in, kv_core = lax.optimization_barrier((gate_in, kv_core))
            kv_sum = kv[0].astype(F32) + sum(x.astype(F32) for x in kv_core)
            kv_chip = [
                lax.ppermute(
                    kv_sum[k].astype(BF16), "branch", branch_target(experts, cores, 0, k)
                )
                for k in range(1, chips)
            ]
        if t == min(5, last):
            gate_in, kv_chip = lax.optimization_barrier((gate_in, kv_chip))
            kv_sum = kv_sum[0] + sum(x.astype(F32) for x in kv_chip)
            merged_kv = (kv_sum / experts).astype(BF16)
            gate_in, merged_kv = lax.optimization_barrier((gate_in, merged_kv))
        if t < last:
            gate_sum = (gate_in.astype(F32) + gates[t].astype(F32)).astype(BF16)
            up_sum = (up_in.astype(F32) + ups[t].astype(F32)).astype(BF16)

    hidden = hidden_rows(
        where, gate_in, up_in, gates[last], ups[last], tails, origin, sizes, parts
    )
    sent = []
    if cores > 1:
        others = down_product(hidden[:parts], weights).astype(BF16)
        others = others.reshape(cores - 1, -1, width)
        sent = [
            lax.ppermute(others[k - 1], "branch", branch_target(experts, cores, k, 0))
            for k in range(1, cores)
        ]
    mixed = down_product(hidden[-parts:], weights)
    mixed, sent = lax.optimization_barrier((mixed, sent))
    mixed = mixed + sum(x.astype(F32) for x in sent)

    mixed = mixed.astype(BF16).reshape(chips * shards, token_count, width)
    groups = [
        [(chip * cores + core) * shards + s for chip in range(chips) for s in range(shards)]
        for core in range(cores)
    ]
    mixed = lax.all_to_all(
        mixed, ("branch", "shard"), split_axis=0, concat_axis=0, axis_index_groups=groups, tiled=True
    )
    return jnp.sum(mixed.astype(F32), axis=0).astype(BF16), merged_kv


def solution(mesh):
    grid = mesh.devices
    order = ring_order(list(grid[0, :]))
    cores = core_count(list(grid[:, 0]))
    return jax.shard_map(
        functools.partial(local, order, cores),
        mesh=mesh,
        in_specs=(
            P(("branch", "shard"), None),
            P(("branch", "shard"), None),
            P(("branch", "shard"), None),
            P("branch", "shard", None),
            P("branch", "shard", None),
            P("branch", "shard", None),
            P("branch", "shard", None),
        ),
        out_specs=(P(("branch", "shard"), None), P("shard", "branch")),
        check_vma=False,
    )
```
